512 devices in a mesh: grp: 16 (over y, z_hi), dev: 32 (over z_lo, x, core).
Axes of the slice: x: 4, y: 4, z: 16 (z_hi: 4, z_lo: 4; z = z_hi * 4 + z_lo), core: 2. Of those that a mesh axis runs over, the one named last changes fastest.
Arguments:
- activations: bfloat16 [3584, 8192], P('grp', 'dev'), may hold values from -6 to 6
- cotangent: bfloat16 [3584, 4096], P('dev', 'grp'), may hold values from -6 to 6
- eigenbasis: bfloat16 [8192, 8192], P('dev'), may hold values from -0.0625 to 0.0625
- second_moment: bfloat16 [8192, 4096], P('dev', 'grp'), may hold values from 0.099609375 to 1
- factor: float32 [8192, 8192], P('grp', 'dev'), may hold values from -1 to 17, as said below
- old_panel: float32 [8192, 128], P('dev', 'grp'), may hold values from -6 to 6
Outputs:
- update: bfloat16 [8192, 4096], P('dev', 'grp')
- new_panel: float32 [8192, 128], P(('grp', 'dev'))
The draws below stay inside these ranges and needn't reach their ends.
Inputs may be any that keep to these rules, and one draw needn't show every extreme that they name: `factor`: symmetric.
All inputs are finite; a program needn't handle non-finite values.
Results may differ from the reference program's by a relative error of at most 0.025.
Values may be sent and summed in bfloat16 or wider, within the bound.
A program may use at most 64 MiB of HBM per device.

```python
import math
import jax
import jax.numpy as jnp
from jax import lax

D = 8192
COLS = 4096
PANEL = 128
TOKENS = 3584
N_DEV = 32


def draw_factor(key, part):
    key = jax.random.fold_in(key, 11)
    noise_key, diag_key = jax.random.split(key)
    noise = jax.random.uniform(noise_key, (D, D), jnp.float32, -1.0, 1.0)
    symmetric = (noise + noise.T) * (3.0 / math.sqrt(D))
    top = jnp.log(10.0)
    levels = 0.5 * jnp.exp(jax.random.uniform(diag_key, (D,), jnp.float32, 0.0, 1.0) * top)
    return symmetric + jnp.diag(levels)


def block_levels(own_key, shape, shards, smallest, top_value):
    factor_of, own = 1.0, jax.random.fold_in(own_key, 6)
    for dim, blocks in shards:
        draws = jnp.exp(jax.random.uniform(jax.random.fold_in(own, dim), (blocks,), jnp.float32, smallest / len(shards), top_value / len(shards)))
        factor_of = factor_of * jnp.repeat(draws, shape[dim] // blocks).reshape([-1 if axis == dim else 1 for axis in range(len(shape))])
    return factor_of


def normal_values(rng, dims, deviation, bound, cuts=(), kind=jnp.bfloat16):
    entries = deviation * jax.random.normal(rng, dims, jnp.float32)
    if cuts:
        entries = entries * block_levels(rng, dims, cuts, -0.22, 0.18)
    return jnp.clip(entries, -bound, bound).astype(kind)


def setup_inputs(seed: int = 0) -> dict:
    arg_keys = jax.random.split(jax.random.key(seed), 7)
    return {
        "activations": normal_values(arg_keys[0], (TOKENS, D), 1.0, 6.0, ((0, 16), (1, 32))),
        "cotangent": normal_values(arg_keys[1], (TOKENS, COLS), 1.0, 6.0, ((0, 32), (1, 16))),
        "eigenbasis": normal_values(arg_keys[2], (D, D), D ** -0.5, 0.0625, ((0, 32),)),
        "second_moment": jnp.clip(jnp.exp(math.log(1.0) - 2.306499 * jax.random.uniform(arg_keys[3], (D, COLS), jnp.float32) ** block_levels(arg_keys[3], (D, COLS), ((0, 32), (1, 16)), -0.2, 0.2)), 0.099609375, 1.0).astype(jnp.bfloat16),
        "factor": draw_factor(jax.random.fold_in(arg_keys[6], 71), 0),
        "old_panel": normal_values(arg_keys[5], (D, PANEL), 1.0, 6.0, ((0, 32), (1, 16)), jnp.float32),
    }


damping = 0.01

def reference(activations, cotangent, eigenbasis, second_moment, factor, old_panel):
    blocks = D // N_DEV
    act_blocks = activations.reshape(TOKENS, N_DEV, blocks).transpose(1, 0, 2)
    basis_blocks = eigenbasis.reshape(N_DEV, blocks, D)

    def add_block(total, pair):
        part = jnp.dot(pair[0].astype(jnp.float32), pair[1].astype(jnp.float32), preferred_element_type=jnp.float32)
        part = lax.optimization_barrier(part.astype(jnp.bfloat16))
        return (total + part.astype(jnp.float32), None)
    summed, _ = lax.scan(add_block, jnp.zeros((TOKENS, D), jnp.float32), (act_blocks, basis_blocks))
    rotated_tokens = summed.astype(jnp.bfloat16)
    moment = jnp.dot(rotated_tokens.T.astype(jnp.float32), cotangent.astype(jnp.float32), preferred_element_type=jnp.float32)
    scaled = (moment / TOKENS / (second_moment.astype(jnp.float32) + damping)).astype(jnp.bfloat16)
    update = jnp.dot(eigenbasis.astype(jnp.float32), scaled.astype(jnp.float32), preferred_element_type=jnp.float32).astype(jnp.bfloat16)
    image = jnp.dot(factor, old_panel, precision=lax.Precision.HIGHEST)
    gram = jnp.dot(image.T, image, precision=lax.Precision.HIGHEST) / D
    lower = jnp.linalg.cholesky(gram)
    new_panel = lax.linalg.triangular_solve(lower, image, left_side=False, lower=True, transpose_a=True)
    return (update, new_panel)
```

```python
import jax
import jax.numpy as jnp
from jax import lax
from jax.experimental import pallas as pl
from jax.experimental.pallas import tpu as pltpu
from jax.sharding import PartitionSpec as P

D = 8192
TOKENS = 3584
PANEL = 128
DAMPING = 0.01
MESH = pl.DeviceIdType.MESH
F32, BF16 = jnp.float32, jnp.bfloat16
HIGHEST = lax.Precision.HIGHEST

N_COPIES = 144


def dot(a, b, dims, precision=None):
    return lax.dot_general(a, b, (dims, ((), ())), precision=precision, preferred_element_type=F32)


def rel(i, o):
    return lax.rem(i + o, 4)


def kernel(
    a_ref, c_ref, q_hbm, v_ref, f_hbm, p_ref, upd_ref, new_ref,
    q, f, tok, cot, pan, scale, gt,
    send_c, recv_c, out2, recv2, out1p, out1m, recv1m, recv1p, out_z, recv_z, total, s, acc,
    im_part, im_c, im_s, im_x, im_xs, im_z,
    gr, gr_c, gr_h, gr_x, gr_q, gr_l, gr_l2, gr_y, gr_y2, gr_z, gr_full, chol_a, chol_b,
    send_sem, recv_sem, local_sem,
):
    grp, dev = lax.axis_index("grp"), lax.axis_index("dev")
    y, h = grp // 4, lax.rem(grp, 4)
    c = lax.rem(dev, 2)
    x = lax.rem(dev // 2, 4)
    z = dev // 8
    other = 1 - c

    def at(yy=y, hh=h, zz=z, xx=x, cc=c):
        return (yy * 4 + hh, (zz * 4 + xx) * 2 + cc)

    core_peer = at(cc=other)
    x_peer = {o: at(xx=rel(x, o)) for o in (1, 2, 3)}
    z_peer = {o: at(zz=rel(z, o)) for o in (1, 2, 3)}
    y_peer = {o: at(yy=rel(y, o)) for o in (1, 2, 3)}
    h_peer = {o: at(hh=rel(h, o)) for o in (1, 2, 3)}
    peers = [core_peer]
    for table in (x_peer, z_peer, y_peer, h_peer):
        peers += [table[o] for o in (1, 2, 3)]

    barrier = pltpu.get_barrier_semaphore()
    for peer in peers:
        pl.semaphore_signal(barrier, inc=1, device_id=peer, device_id_type=MESH)
    load_q = pltpu.make_async_copy(q_hbm, q, local_sem.at[0])
    load_f = pltpu.make_async_copy(f_hbm, f, local_sem.at[1])
    load_f.start()
    load_q.start()
    pl.semaphore_wait(barrier, len(peers))

    started = []

    def push(src, dst, peer):
        n = len(started)
        copy = pltpu.make_async_remote_copy(
            src_ref=src, dst_ref=dst, send_sem=send_sem.at[n], recv_sem=recv_sem.at[n],
            device_id=peer, device_id_type=MESH,
        )
        copy.start()
        started.append(copy)
        return copy

    pan_h = {o: push(p_ref, pan.at[h, y], h_peer[o]) for o in (1, 2, 3)}
    cot_x, cot_z, cot_f, cot_c = {}, {}, {}, {}
    for o in (2, 1, 3):
        cot_z[o] = push(c_ref, cot.at[x, z, c], z_peer[o])
    for o in (1, 3):
        cot_x[o, 0] = push(c_ref, cot.at[x, z, c], x_peer[o])
    tok_h, tok_y, tok_f = {}, {}, {}
    for o in (2, 1, 3):
        tok_h[o] = push(a_ref, tok.at[h, y], h_peer[o])
    for o in (1, 3):
        tok_y[o, 0] = push(a_ref, tok.at[h, y], y_peer[o])
    tok[h, y] = a_ref[...]
    cot[x, z, c] = c_ref[...]
    pan[h, y] = p_ref[...]
    scale[...] = (1.0 / TOKENS) / (v_ref[...].astype(F32) + DAMPING)

    for o in (1, 2, 3):
        pan_h[o].wait_recv()
    pan_y = {o: push(pan.at[:, y], pan.at[:, y], y_peer[o]) for o in (1, 2, 3)}

    for o in (1, 3, 2):
        cot_z[o].wait_recv()
        zz = rel(z, 4 - o)
        for ox in (1, 3):
            cot_x[ox, 4 - o] = push(cot.at[x, zz, c], cot.at[x, zz, c], x_peer[ox])
    cot_c[0] = push(cot.at[x, :, c], cot.at[x, :, c], core_peer)

    for o in (1, 2, 3):
        pan_y[o].wait_recv()
    load_f.wait()
    pan_t = pan[...].reshape(4, 4, 8, 256).transpose(1, 0, 2, 3).reshape(PANEL, 256)
    im_part[...] = dot(f[...], pan_t, ((1,), (1,)), HIGHEST).reshape(4, 4, 2, 16, PANEL)
    im_core = push(im_part.at[:, :, other], im_c, core_peer)

    for j in (0, 3, 1, 2):
        zz = rel(z, j)
        cot_x[1, j].wait_recv()
        if j in (0, 1):
            cot_f[j] = push(cot.at[rel(x, 3), zz, c], cot.at[rel(x, 3), zz, c], x_peer[1])
        cot_x[3, j].wait_recv()
        if j in (3, 2):
            cot_f[j] = push(cot.at[rel(x, 1), zz, c], cot.at[rel(x, 1), zz, c], x_peer[3])
    for o in (1, 3):
        cot_c[o] = push(cot.at[rel(x, o), :, c], cot.at[rel(x, o), :, c], core_peer)

    im_core.wait_recv()
    im_s[...] = im_part[:, :, c] + im_c[...]
    im_xc = {o: push(im_s.at[:, rel(x, o)], im_x.at[o], x_peer[o]) for o in (1, 2, 3)}

    for j in (0, 3, 1, 2):
        cot_f[j].wait_recv()
    cot_c[2] = push(cot.at[rel(x, 2), :, c], cot.at[rel(x, 2), :, c], core_peer)

    for o in (1, 2, 3):
        im_xc[o].wait_recv()
    im_xs[...] = im_s[:, x] + im_x[1] + im_x[2] + im_x[3]
    im_zc = {o: push(im_xs.at[rel(z, o)], im_z.at[o], z_peer[o]) for o in (1, 2, 3)}

    for o in (1, 3, 2):
        tok_h[o].wait_recv()
        hh = rel(h, 4 - o)
        for oy in (1, 3):
            tok_y[oy, 4 - o] = push(tok.at[hh, y], tok.at[hh, y], y_peer[oy])

    for o in (1, 2, 3):
        im_zc[o].wait_recv()
    image = im_xs[z] + im_z[1] + im_z[2] + im_z[3]
    gr[...] = dot(image, image, ((0,), (0,)), HIGHEST) * (1.0 / D)
    chol_b[...] = jnp.concatenate([image, jnp.zeros((PANEL - 16, PANEL), F32)], axis=0).T
    gr_core = push(gr.at[pl.ds(pl.multiple_of(other * 64, 64), 64)], gr_c, core_peer)

    for j in (0, 3, 1, 2):
        hh = rel(h, j)
        tok_y[1, j].wait_recv()
        if j in (0, 1):
            tok_f[j] = push(tok.at[hh, rel(y, 3)], tok.at[hh, rel(y, 3)], y_peer[1])
        tok_y[3, j].wait_recv()
        if j in (3, 2):
            tok_f[j] = push(tok.at[hh, rel(y, 1)], tok.at[hh, rel(y, 1)], y_peer[3])

    gr_core.wait_recv()
    gr_h[...] = gr[pl.ds(pl.multiple_of(c * 64, 64), 64), :] + gr_c[...]
    gr_xc = {
        o: push(gr_h.at[pl.ds(pl.multiple_of(rel(x, o) * 16, 16), 16)], gr_x.at[o], x_peer[o])
        for o in (1, 2, 3)
    }

    for j in (0, 3, 1, 2):
        tok_f[j].wait_recv()
    for o in (0, 1, 2, 3):
        cot_c[o].wait_recv()
    load_q.wait()

    gt[...] = dot(
        cot[...].reshape(TOKENS, 256), tok[...].reshape(TOKENS, 256), ((0,), (0,))
    ).astype(BF16)

    def block(ox, oz, cc):
        start = ((rel(z, oz) * 4 + rel(x, ox)) * 2 + cc) * 256
        return dot(gt[...], q[:, pl.ds(pl.multiple_of(start, 256), 256)], ((1,), (0,)))

    order = (2, 1, 3, 0)
    core = {}
    for ox in (2, 1, 3, 0):
        for j in range(4):
            send_c[ox, j] = block(ox, order[j], other).astype(BF16)
            core[ox, j] = push(send_c.at[ox, j], recv_c.at[ox, j], core_peer)

    def pair_sum(ox, j):
        own = block(ox, order[j], c)
        core[ox, j].wait_recv()
        return own + recv_c[ox, j].astype(F32)

    far, plus, minus, near = {}, {}, {}, {}

    def send_far(j):
        out2[j] = pair_sum(2, j).astype(BF16)
        far[j] = push(out2.at[j], recv2.at[j], x_peer[1 if j < 2 else 3])

    def send_plus(j):
        v = pair_sum(1, j)
        if j < 2:
            far[j].wait_recv()
            v = v + recv2[j].astype(F32)
        out1p[j] = v.astype(BF16)
        plus[j] = push(out1p.at[j], recv1m.at[j], x_peer[1])

    def send_minus(j):
        v = pair_sum(3, j)
        if j >= 2:
            far[j].wait_recv()
            v = v + recv2[j].astype(F32)
        out1m[j] = v.astype(BF16)
        minus[j] = push(out1m.at[j], recv1p.at[j], x_peer[3])

    send_far(0)
    send_minus(0)
    send_far(1)
    send_minus(1)
    send_far(2)
    send_far(3)
    for o in (1, 2, 3):
        gr_xc[o].wait_recv()
    gr_q[...] = gr_h[pl.ds(pl.multiple_of(x * 16, 16), 16), :] + gr_x[1] + gr_x[2] + gr_x[3]
    gr_zc = {o: push(gr_q, gr_l.at[o], z_peer[o]) for o in (1, 2, 3)}
    send_plus(0)
    send_plus(1)
    send_plus(2)
    send_minus(2)
    send_plus(3)
    send_minus(3)
    for o in (1, 2, 3):
        gr_zc[o].wait_recv()
    gr_l2[...] = gr_q[...] + gr_l[1] + gr_l[2] + gr_l[3]
    gr_yc = {o: push(gr_l2, gr_y.at[o], y_peer[o]) for o in (1, 2, 3)}

    for j in range(4):
        v = pair_sum(0, j)
        plus[j].wait_recv()
        v = v + recv1m[j].astype(F32)
        minus[j].wait_recv()
        v = v + recv1p[j].astype(F32)
        if order[j]:
            out_z[j] = v.astype(BF16)
            near[j] = push(out_z.at[j], recv_z.at[j], z_peer[order[j]])
        else:
            total[...] = v
        if j == 1:
            for o in (1, 2, 3):
                gr_yc[o].wait_recv()
            gr_y2[...] = gr_l2[...] + gr_y[1] + gr_y[2] + gr_y[3]
            gr_hc = {o: push(gr_y2, gr_z.at[o], h_peer[o]) for o in (1, 2, 3)}
    moment = total[...]
    for j in range(3):
        near[j].wait_recv()
        moment = moment + recv_z[j].astype(F32)
    s[0, 0, c] = (moment.T * scale[...]).astype(BF16)

    s_z, s_x, s_f, s_c = {}, {}, {}, {}
    mine = s.at[0, 0, c]
    for o in (2, 1, 3):
        s_z[o] = push(mine, s.at[0, 4 - o, c], z_peer[o])
    for o in (1, 3):
        s_x[o, 0] = push(mine, s.at[4 - o, 0, c], x_peer[o])
    s_c[0, 0] = push(mine, mine, core_peer)

    for o in (1, 2, 3):
        gr_hc[o].wait_recv()
    lo = pl.ds(pl.multiple_of(c * 64 + x * 16, 16), 16)
    gr_full[lo, :] = gr_y2[...] + gr_z[1] + gr_z[2] + gr_z[3]
    gr_xg = {o: push(gr_full.at[lo], gr_full.at[lo], x_peer[o]) for o in (1, 2, 3)}

    for o in (1, 3, 2):
        s_z[o].wait_recv()
        j = 4 - o
        for ox in (1, 3):
            s_x[ox, j] = push(s.at[0, j, c], s.at[4 - ox, j, c], x_peer[ox])
        s_c[0, j] = push(s.at[0, j, c], s.at[0, j, c], core_peer)

    for o in (1, 2, 3):
        gr_xg[o].wait_recv()
    half = pl.ds(pl.multiple_of(c * 64, 64), 64)
    gr_cg = push(gr_full.at[half], gr_full.at[half], core_peer)

    lane = lax.broadcasted_iota(jnp.int32, (8, PANEL), 1)
    row = lax.broadcasted_iota(jnp.int32, (8, PANEL), 0)

    def eliminate(b, carry):
        k0 = pl.multiple_of(b * 8, 8)
        r = chol_a[pl.ds(k0, 8), :]
        w = chol_b[pl.ds(k0, 8), :]
        r = pltpu.roll(r, lax.rem(PANEL - k0, PANEL), 1)
        for i in range(8):
            column = r[:, i : i + 1]
            pivot = column[i : i + 1, :]
            inv = lax.rsqrt(pivot)
            inv = inv * (1.5 - 0.5 * pivot * inv * inv)
            factor = column * inv
            r_row = r[i : i + 1, :] * inv
            w_row = w[i : i + 1, :] * inv
            r = jnp.where(row == i, r_row, jnp.where(row > i, r - factor * r_row, r))
            w = jnp.where(row == i, w_row, jnp.where(row > i, w - factor * w_row, w))
        r = pltpu.roll(r, k0, 1)
        r = jnp.where(lane >= k0 + 8, r, 0.0)
        chol_a[...] -= dot(r, r, ((0,), (0,)), HIGHEST)
        chol_b[...] -= dot(r, w, ((0,), (0,)), HIGHEST)
        chol_b[pl.ds(k0, 8), :] = w
        return carry

    def add_pair(ox, oz, first=False):
        start = ((rel(z, oz) * 4 + rel(x, ox)) * 2) * 256
        part = dot(
            q[:, pl.ds(pl.multiple_of(start, 512), 512)], s[ox, oz].reshape(512, 256), ((1,), (0,))
        )
        if first:
            acc[...] = part
        else:
            acc[...] += part

    gr_cg.wait_recv()
    chol_a[...] = gr_full[...]

    step = 0
    for j in (0, 3, 1, 2):
        s_x[1, j].wait_recv()
        if j in (0, 1):
            s_f[j] = push(s.at[3, j, c], s.at[2, j, c], x_peer[1])
        s_c[3, j] = push(s.at[3, j, c], s.at[3, j, c], core_peer)
        s_x[3, j].wait_recv()
        if j in (3, 2):
            s_f[j] = push(s.at[1, j, c], s.at[2, j, c], x_peer[3])
        s_c[1, j] = push(s.at[1, j, c], s.at[1, j, c], core_peer)
        s_c[0, j].wait_recv()
        add_pair(0, j, j == 0)
        lax.fori_loop(2 * step, 2 * step + 2, eliminate, 0)
        step += 1
    for j in (0, 3, 1, 2):
        s_f[j].wait_recv()
        s_c[2, j] = push(s.at[2, j, c], s.at[2, j, c], core_peer)
        for ox in (1, 3):
            s_c[ox, j].wait_recv()
            add_pair(ox, j)
        lax.fori_loop(2 * step, 2 * step + 2, eliminate, 0)
        step += 1
    new_ref[...] = chol_b[...].T[:16, :]
    for j in (0, 3, 1, 2):
        s_c[2, j].wait_recv()
        add_pair(2, j)
    upd_ref[...] = acc[...].astype(BF16)
    for copy in started:
        copy.wait_send()
    assert len(started) <= N_COPIES


def body(activations, cotangent, eigenbasis, second_moment, factor, old_panel):
    vmem = pl.BlockSpec(memory_space=pltpu.VMEM)
    hbm = pl.BlockSpec(memory_space=pl.ANY)
    tile = (256, 256)
    part = (16, PANEL)
    scratch = [
        pltpu.VMEM((256, D), BF16),
        pltpu.VMEM((512, 256), F32),
        pltpu.VMEM((4, 4, 224, 256), BF16),
        pltpu.VMEM((4, 4, 2, 112, 256), BF16),
        pltpu.VMEM((4, 4, 8, 256), F32),
        pltpu.VMEM(tile, F32),
        pltpu.VMEM(tile, BF16),
        pltpu.VMEM((4, 4) + tile, BF16),
        pltpu.VMEM((4, 4) + tile, BF16),
        pltpu.VMEM((4,) + tile, BF16),
        pltpu.VMEM((4,) + tile, BF16),
        pltpu.VMEM((4,) + tile, BF16),
        pltpu.VMEM((4,) + tile, BF16),
        pltpu.VMEM((4,) + tile, BF16),
        pltpu.VMEM((4,) + tile, BF16),
        pltpu.VMEM((4,) + tile, BF16),
        pltpu.VMEM((4,) + tile, BF16),
        pltpu.VMEM(tile, F32),
        pltpu.VMEM((4, 4, 2) + tile, BF16),
        pltpu.VMEM(tile, F32),
        pltpu.VMEM((4, 4, 2) + part, F32),
        pltpu.VMEM((4, 4) + part, F32),
        pltpu.VMEM((4, 4) + part, F32),
        pltpu.VMEM((4, 4) + part, F32),
        pltpu.VMEM((4,) + part, F32),
        pltpu.VMEM((4,) + part, F32),
        pltpu.VMEM((PANEL, PANEL), F32),
        pltpu.VMEM((64, PANEL), F32),
        pltpu.VMEM((64, PANEL), F32),
        pltpu.VMEM((4,) + part, F32),
        pltpu.VMEM(part, F32),
        pltpu.VMEM((4,) + part, F32),
        pltpu.VMEM(part, F32),
        pltpu.VMEM((4,) + part, F32),
        pltpu.VMEM(part, F32),
        pltpu.VMEM((4,) + part, F32),
        pltpu.VMEM((PANEL, PANEL), F32),
        pltpu.VMEM((PANEL, PANEL), F32),
        pltpu.VMEM((PANEL, PANEL), F32),
        pltpu.SemaphoreType.DMA((N_COPIES,)),
        pltpu.SemaphoreType.DMA((N_COPIES,)),
        pltpu.SemaphoreType.DMA((2,)),
    ]
    return pl.pallas_call(
        kernel,
        out_shape=(
            jax.ShapeDtypeStruct(tile, BF16),
            jax.ShapeDtypeStruct(part, F32),
        ),
        in_specs=[vmem, vmem, hbm, vmem, hbm, vmem],
        out_specs=(vmem, vmem),
        scratch_shapes=scratch,
        compiler_params=pltpu.CompilerParams(
            collective_id=0, has_side_effects=True, vmem_limit_bytes=48 * 1024 * 1024
        ),
    )(activations, cotangent, eigenbasis, second_moment, factor, old_panel.T)


def solution(mesh):
    return jax.shard_map(
        body,
        mesh=mesh,
        in_specs=(
            P("grp", "dev"),
            P("dev", "grp"),
            P("dev", None),
            P("dev", "grp"),
            P("grp", "dev"),
            P("dev", "grp"),
        ),
        out_specs=(P("dev", "grp"), P(("grp", "dev"), None)),
        check_vma=False,
    )
```

```python
import jax
import jax.numpy as jnp
from jax import lax
from jax.experimental import pallas as pl
from jax.experimental.pallas import tpu as pltpu
from jax.sharding import PartitionSpec as P

D = 8192
TOKENS = 3584
PANEL = 128
DAMPING = 0.01
MESH = pl.DeviceIdType.MESH
F32, BF16 = jnp.float32, jnp.bfloat16
HIGHEST = lax.Precision.HIGHEST

N_COPIES = 176


def dot(a, b, dims, precision=None):
    return lax.dot_general(a, b, (dims, ((), ())), precision=precision, preferred_element_type=F32)


def rel(i, o):
    return lax.rem(i + o, 4)


def kernel(
    a_hbm, c_hbm, q_hbm, v_hbm, f_hbm, p_hbm, upd_ref, new_ref,
    q, f, v, tok, cot, pan, scale, gt_sum, gt,
    send_c, recv_c, out2, recv2, out1p, out1m, recv1m, recv1p, out_z, recv_z, total, s, acc,
    im_part, im_c, im_s, im_x, im_xs, im_z,
    gr, gr_c, gr_h, gr_x, gr_q, gr_l, gr_l2, gr_y, gr_y2, gr_z, gr_full, chol,
    send_sem, recv_sem, local_sem,
):
    grp, dev = lax.axis_index("grp"), lax.axis_index("dev")
    y, h = grp // 4, lax.rem(grp, 4)
    c = lax.rem(dev, 2)
    x = lax.rem(dev // 2, 4)
    z = dev // 8
    other = 1 - c

    def at(yy=y, hh=h, zz=z, xx=x, cc=c):
        return (yy * 4 + hh, (zz * 4 + xx) * 2 + cc)

    core_peer = at(cc=other)
    x_peer = {o: at(xx=rel(x, o)) for o in (1, 2, 3)}
    z_peer = {o: at(zz=rel(z, o)) for o in (1, 2, 3)}
    y_peer = {o: at(yy=rel(y, o)) for o in (1, 2, 3)}
    h_peer = {o: at(hh=rel(h, o)) for o in (1, 2, 3)}
    peers = [core_peer]
    for table in (x_peer, z_peer, y_peer, h_peer):
        peers += [table[o] for o in (1, 2, 3)]

    barrier = pltpu.get_barrier_semaphore()
    for peer in peers:
        pl.semaphore_signal(barrier, inc=1, device_id=peer, device_id_type=MESH)

    pairs = (
        (a_hbm, tok.at[h, y]), (c_hbm, cot.at[x, z, c]), (p_hbm, pan.at[h, y]),
        (v_hbm, v), (f_hbm, f), (q_hbm, q),
    )
    loads = [pltpu.make_async_copy(src, dst, local_sem.at[n]) for n, (src, dst) in enumerate(pairs)]
    for load in loads:
        load.start()
    for load in loads[:3]:
        load.wait()
    pl.semaphore_wait(barrier, len(peers))

    started, received = [], []

    def push(src, dst, peer):
        n = len(started)
        copy = pltpu.make_async_remote_copy(
            src_ref=src, dst_ref=dst, send_sem=send_sem.at[n], recv_sem=recv_sem.at[n],
            device_id=peer, device_id_type=MESH,
        )
        copy.start()
        started.append(copy)
        return copy

    def need(*copies):
        for copy in copies:
            assert id(copy) not in received
            received.append(id(copy))
            copy.wait_recv()

    def tok_push(hh, yy, k, peer):
        piece = tok.at[hh, yy, k]
        return push(piece, piece, peer)

    tok_h, tok_y, tok_yf = {}, {}, {}

    def tok_to_y(j, k):
        for o in (1, 3):
            tok_y[o, j, k] = tok_push(rel(h, j), y, k, y_peer[o])

    def tok_forward(j, k):
        o = (1, 3)[k]
        need(tok_y[o, j, k])
        tok_yf[j, k] = tok_push(rel(h, j), rel(y, 4 - o), k, y_peer[o])

    cot_x, cot_z, cot_f, cot_c = {}, {}, {}, {}

    def cot_push(xx, zz, peer):
        return push(cot.at[xx, zz, c], cot.at[xx, zz, c], peer)

    def cot_forward(j):
        zz = rel(z, j)
        need(cot_x[1, j], cot_x[3, j])
        o = 1 if j < 2 else 3
        cot_f[j] = cot_push(rel(x, 4 - o), zz, x_peer[o])

    def cot_pair(o):
        part = cot.at[rel(x, o), :, c]
        cot_c[o] = push(part, part, core_peer)

    pan_h = {o: push(pan.at[h, y], pan.at[h, y], h_peer[o]) for o in (2, 1, 3)}
    for o, k in ((1, 0), (3, 1)):
        tok_h[o, k] = tok_push(h, y, k, h_peer[o])
    for o in (2, 1, 3):
        cot_z[o] = cot_push(x, z, z_peer[o])
    for o, k in ((1, 1), (3, 0)):
        tok_h[o, k] = tok_push(h, y, k, h_peer[o])
    for k in (0, 1):
        tok_to_y(0, k)
    for o in (1, 3):
        cot_x[o, 0] = cot_push(x, z, x_peer[o])
    loads[3].wait()
    scale[...] = (1.0 / TOKENS) / (v[...].astype(F32) + DAMPING)

    tok_forward(0, 0)
    tok_forward(0, 1)
    need(*pan_h.values())
    pan_y = {o: push(pan.at[:, y], pan.at[:, y], y_peer[o]) for o in (2, 1, 3)}
    for o in (1, 3, 2):
        need(cot_z[o])
        for ox in (1, 3):
            cot_x[ox, 4 - o] = cot_push(x, rel(z, 4 - o), x_peer[ox])
    cot_pair(0)
    cot_forward(0)
    tok_hf = {}
    for o, k in ((1, 0), (3, 1)):
        need(tok_h[o, k])
        tok_hf[k] = tok_push(rel(h, 4 - o), y, k, h_peer[o])
        tok_to_y(4 - o, k)
    need(*pan_y.values())
    loads[4].wait()
    pan_t = pan[...].reshape(4, 4, 8, 256).transpose(1, 0, 2, 3).reshape(PANEL, 256)
    im_part[...] = dot(f[...], pan_t, ((1,), (1,)), HIGHEST).reshape(4, 4, 2, 16, PANEL)
    im_core = push(im_part.at[:, :, other], im_c, core_peer)
    for j in (3, 1, 2):
        cot_forward(j)
    cot_pair(1)
    cot_pair(3)
    tok_forward(3, 0)
    tok_forward(1, 1)
    need(im_core)
    im_s[...] = im_part[:, :, c] + im_c[...]
    im_xc = {o: push(im_s.at[:, rel(x, o)], im_x.at[o], x_peer[o]) for o in (1, 2, 3)}
    for o, k in ((1, 1), (3, 0)):
        need(tok_h[o, k])
        tok_to_y(4 - o, k)
    need(*cot_f.values())
    cot_pair(2)
    need(*im_xc.values())
    im_xs[...] = im_s[:, x] + im_x[1] + im_x[2] + im_x[3]
    im_zc = {o: push(im_xs.at[rel(z, o)], im_z.at[o], z_peer[o]) for o in (1, 2, 3)}
    for k in (0, 1):
        need(tok_hf[k])
        tok_to_y(2, k)
    tok_forward(3, 1)
    tok_forward(1, 0)
    need(*im_zc.values())
    image = im_xs[z] + im_z[1] + im_z[2] + im_z[3]
    gr[...] = dot(image, image, ((0,), (0,)), HIGHEST) * (1.0 / D)
    chol[:, PANEL:] = jnp.concatenate([image, jnp.zeros((PANEL - 16, PANEL), F32)], axis=0).T
    gr_core = push(gr.at[pl.ds(pl.multiple_of(other * 64, 64), 64)], gr_c, core_peer)
    tok_forward(2, 0)
    tok_forward(2, 1)
    need(*cot_c.values())
    need(gr_core)
    gr_h[...] = gr[pl.ds(pl.multiple_of(c * 64, 64), 64), :] + gr_c[...]
    gr_xc = {
        o: push(gr_h.at[pl.ds(pl.multiple_of(rel(x, o) * 16, 16), 16)], gr_x.at[o], x_peer[o])
        for o in (1, 2, 3)
    }

    for j in (0, 3, 1, 2):
        need(tok_y[3, j, 0], tok_y[1, j, 1], tok_yf[j, 0], tok_yf[j, 1])
        hh = rel(h, j)
        part = dot(cot[hh].reshape(896, 256), tok[hh].reshape(896, 256), ((0,), (0,)))
        if j == 0:
            gt_sum[...] = part
        elif j == 2:
            gt[...] = (gt_sum[...] + part).astype(BF16).reshape(2, 128, 256)
        else:
            gt_sum[...] += part
    loads[5].wait()

    order = (2, 1, 3, 0)

    def block(k, ox, j, cc):
        start = ((rel(z, order[j]) * 4 + rel(x, ox)) * 2 + cc) * 256
        return dot(gt[k], q[:, pl.ds(pl.multiple_of(start, 256), 256)], ((1,), (0,)))

    core, far, plus, minus, near = {}, {}, {}, {}, {}

    def send_core(k):
        for ox in (2, 3, 1, 0):
            for j in range(4):
                send_c[k, ox, j] = block(k, ox, j, other).astype(BF16)
            core[k, ox] = push(send_c.at[k, ox], recv_c.at[k, ox], core_peer)

    def pair_sum(k, ox, j):
        return block(k, ox, j, c) + recv_c[k, ox, j].astype(F32)

    def send_far(k, j):
        out2[k, j] = pair_sum(k, 2, j).astype(BF16)
        far[k, j] = push(out2.at[k, j], recv2.at[k, j], x_peer[1 if j < 2 else 3])

    def send_plus(k, j):
        total_j = pair_sum(k, 1, j)
        if j < 2:
            need(far[k, j])
            total_j = total_j + recv2[k, j].astype(F32)
        out1p[k, j] = total_j.astype(BF16)
        plus[k, j] = push(out1p.at[k, j], recv1m.at[k, j], x_peer[1])

    def send_minus(k, j):
        total_j = pair_sum(k, 3, j)
        if j >= 2:
            need(far[k, j])
            total_j = total_j + recv2[k, j].astype(F32)
        out1m[k, j] = total_j.astype(BF16)
        minus[k, j] = push(out1m.at[k, j], recv1p.at[k, j], x_peer[3])

    def send_first(k):
        need(core[k, 2])
        for j in (0, 2, 1, 3):
            send_far(k, j)
        need(core[k, 3])
        send_minus(k, 0)
        send_minus(k, 1)
        need(core[k, 1])
        send_plus(k, 2)
        send_plus(k, 3)

    def send_second(k):
        send_plus(k, 0)
        send_minus(k, 2)
        send_plus(k, 1)
        send_minus(k, 3)

    def send_z(k):
        need(core[k, 0])
        for j in range(4):
            total_j = pair_sum(k, 0, j)
            need(plus[k, j], minus[k, j])
            total_j = total_j + recv1m[k, j].astype(F32) + recv1p[k, j].astype(F32)
            if order[j]:
                out_z[k, j] = total_j.astype(BF16)
                near[k, j] = push(out_z.at[k, j], recv_z.at[k, j], z_peer[order[j]])
            else:
                total[k] = total_j

    s_z, s_x, s_f, s_c = {}, {}, {}, {}

    def gather_own(k):
        moment = total[k]
        for j in range(3):
            need(near[k, j])
            moment = moment + recv_z[k, j].astype(F32)
        s[k, 0, 0, c] = (moment.T * scale[:, k * 128 : (k + 1) * 128]).astype(BF16)
        mine = s.at[k, 0, 0, c]
        for o in (2, 1, 3):
            s_z[k, o] = push(mine, s.at[k, 0, 4 - o, c], z_peer[o])
        for o in (1, 3):
            s_x[k, o, 0] = push(mine, s.at[k, 4 - o, 0, c], x_peer[o])

    def gather_z(k, o):
        need(s_z[k, o])
        j = 4 - o
        for ox in (1, 3):
            s_x[k, ox, j] = push(s.at[k, 0, j, c], s.at[k, 4 - ox, j, c], x_peer[ox])

    def gather_pair(k, ox, lo, hi):
        part = s.at[k, ox, lo:hi, c]
        s_c[k, ox, lo] = push(part, part, core_peer)

    def gather_forward(k, j):
        need(s_x[k, 1, j], s_x[k, 3, j])
        o = 1 if j < 2 else 3
        s_f[k, j] = push(s.at[k, 4 - o, j, c], s.at[k, 2, j, c], x_peer[o])

    def add_blocks(k, ox, lo, hi):
        need(s_c[k, ox, lo])
        for j in range(lo, hi):
            start = ((rel(z, j) * 4 + rel(x, ox)) * 2) * 256
            part = dot(
                q[:, pl.ds(pl.multiple_of(start, 512), 512)],
                s[k, ox, j].reshape(512, 128),
                ((1,), (0,)),
            )
            if j == lo:
                sum_j = part
            else:
                sum_j = sum_j + part
        if ox == 0:
            acc[k] = sum_j
        else:
            acc[k] += sum_j

    lane = lax.broadcasted_iota(jnp.int32, (8, PANEL), 1)
    row = lax.broadcasted_iota(jnp.int32, (8, PANEL), 0)

    def eliminate(b):
        k0 = 8 * b
        r = chol[k0 : k0 + 8, :PANEL]
        w = chol[k0 : k0 + 8, PANEL:]
        for i in range(8):
            column = r[:, k0 + i : k0 + i + 1]
            pivot = column[i : i + 1, :]
            inv = lax.rsqrt(pivot)
            inv = inv * (1.5 - 0.5 * pivot * inv * inv)
            below = column * inv
            r_row = r[i : i + 1, :] * inv
            w_row = w[i : i + 1, :] * inv
            r = jnp.where(row == i, r_row, jnp.where(row > i, r - below * r_row, r))
            w = jnp.where(row == i, w_row, jnp.where(row > i, w - below * w_row, w))
        if b < 15:
            r = jnp.where(lane >= k0 + 8, r, 0.0)
            chol[...] -= dot(r, jnp.concatenate([r, w], axis=1), ((0,), (0,)), HIGHEST)
        chol[k0 : k0 + 8, PANEL:] = w

    send_core(0)
    send_first(0)
    need(*gr_xc.values())
    gr_q[...] = gr_h[pl.ds(pl.multiple_of(x * 16, 16), 16), :] + gr_x[1] + gr_x[2] + gr_x[3]
    gr_zc = {o: push(gr_q, gr_l.at[o], z_peer[o]) for o in (1, 2, 3)}
    send_core(1)
    send_second(0)
    need(*gr_zc.values())
    gr_l2[...] = gr_q[...] + gr_l[1] + gr_l[2] + gr_l[3]
    gr_yc = {o: push(gr_l2, gr_y.at[o], y_peer[o]) for o in (1, 2, 3)}
    send_first(1)
    need(*gr_yc.values())
    gr_y2[...] = gr_l2[...] + gr_y[1] + gr_y[2] + gr_y[3]
    gr_hc = {o: push(gr_y2, gr_z.at[o], h_peer[o]) for o in (1, 2, 3)}
    send_z(0)
    send_second(1)
    need(*gr_hc.values())
    lo = pl.ds(pl.multiple_of(c * 64 + x * 16, 16), 16)
    gr_full[lo, :] = gr_y2[...] + gr_z[1] + gr_z[2] + gr_z[3]
    gr_xg = {o: push(gr_full.at[lo], gr_full.at[lo], x_peer[o]) for o in (1, 2, 3)}
    send_z(1)
    gather_own(0)
    need(*gr_xg.values())
    half = pl.ds(pl.multiple_of(c * 64, 64), 64)
    gr_cg = push(gr_full.at[half], gr_full.at[half], core_peer)
    gather_own(1)
    need(gr_cg)
    chol[:, :PANEL] = gr_full[...]

    steps = iter(range(16))
    for k in (0, 1):
        for o in (1, 3, 2):
            gather_z(k, o)
            eliminate(next(steps))
        gather_pair(k, 0, 0, 4)
        for j in (0, 3, 1, 2):
            gather_forward(k, j)
            eliminate(next(steps))
        gather_pair(k, 1, 0, 4)
        gather_pair(k, 3, 0, 4)
        add_blocks(k, 0, 0, 4)
        if k == 1:
            for b in steps:
                eliminate(b)
            new_ref[...] = chol[:, PANEL:].T[:16, :]
            add_blocks(0, 1, 0, 4)
            add_blocks(0, 3, 0, 4)
    for k in (0, 1):
        need(s_f[k, 0], s_f[k, 1])
        gather_pair(k, 2, 0, 2)
        need(s_f[k, 2], s_f[k, 3])
        gather_pair(k, 2, 2, 4)
    add_blocks(1, 1, 0, 4)
    add_blocks(1, 3, 0, 4)
    for k in (0, 1):
        add_blocks(k, 2, 0, 2)
        add_blocks(k, 2, 2, 4)
        upd_ref[:, k * 128 : (k + 1) * 128] = acc[k].astype(BF16)
    for copy in started:
        copy.wait_send()
    assert len(started) <= N_COPIES
    assert len(started) == len(received)


def body(activations, cotangent, eigenbasis, second_moment, factor, old_panel):
    vmem = pl.BlockSpec(memory_space=pltpu.VMEM)
    hbm = pl.BlockSpec(memory_space=pl.ANY)
    tile = (128, 256)
    part = (16, PANEL)
    scratch = [
        pltpu.VMEM((256, D), BF16),
        pltpu.VMEM((512, 256), F32),
        pltpu.VMEM((256, 256), BF16),
        pltpu.VMEM((4, 4, 2, 112, 256), BF16),
        pltpu.VMEM((4, 4, 2, 112, 256), BF16),
        pltpu.VMEM((4, 4, 8, 256), F32),
        pltpu.VMEM((256, 256), F32),
        pltpu.VMEM((256, 256), F32),
        pltpu.VMEM((2,) + tile, BF16),
        pltpu.VMEM((2, 4, 4) + tile, BF16),
        pltpu.VMEM((2, 4, 4) + tile, BF16),
        pltpu.VMEM((2, 4) + tile, BF16),
        pltpu.VMEM((2, 4) + tile, BF16),
        pltpu.VMEM((2, 4) + tile, BF16),
        pltpu.VMEM((2, 4) + tile, BF16),
        pltpu.VMEM((2, 4) + tile, BF16),
        pltpu.VMEM((2, 4) + tile, BF16),
        pltpu.VMEM((2, 3) + tile, BF16),
        pltpu.VMEM((2, 3) + tile, BF16),
        pltpu.VMEM((2,) + tile, F32),
        pltpu.VMEM((2, 4, 4, 2, 256, 128), BF16),
        pltpu.VMEM((2, 256, 128), F32),
        pltpu.VMEM((4, 4, 2) + part, F32),
        pltpu.VMEM((4, 4) + part, F32),
        pltpu.VMEM((4, 4) + part, F32),
        pltpu.VMEM((4, 4) + part, F32),
        pltpu.VMEM((4,) + part, F32),
        pltpu.VMEM((4,) + part, F32),
        pltpu.VMEM((PANEL, PANEL), F32),
        pltpu.VMEM((64, PANEL), F32),
        pltpu.VMEM((64, PANEL), F32),
        pltpu.VMEM((4,) + part, F32),
        pltpu.VMEM(part, F32),
        pltpu.VMEM((4,) + part, F32),
        pltpu.VMEM(part, F32),
        pltpu.VMEM((4,) + part, F32),
        pltpu.VMEM(part, F32),
        pltpu.VMEM((4,) + part, F32),
        pltpu.VMEM((PANEL, PANEL), F32),
        pltpu.VMEM((PANEL, 2 * PANEL), F32),
        pltpu.SemaphoreType.DMA((N_COPIES,)),
        pltpu.SemaphoreType.DMA((N_COPIES,)),
        pltpu.SemaphoreType.DMA((6,)),
    ]
    return pl.pallas_call(
        kernel,
        out_shape=(
            jax.ShapeDtypeStruct((256, 256), BF16),
            jax.ShapeDtypeStruct(part, F32),
        ),
        in_specs=[hbm] * 6,
        out_specs=(vmem, vmem),
        scratch_shapes=scratch,
        compiler_params=pltpu.CompilerParams(
            collective_id=0, has_side_effects=True, vmem_limit_bytes=60 * 1024 * 1024
        ),
    )(
        activations.reshape(2, 112, 256), cotangent, eigenbasis, second_moment, factor, old_panel.T
    )


def solution(mesh):
    return jax.shard_map(
        body,
        mesh=mesh,
        in_specs=(
            P("grp", "dev"),
            P("dev", "grp"),
            P("dev", None),
            P("dev", "grp"),
            P("grp", "dev"),
            P("dev", "grp"),
        ),
        out_specs=(P("dev", "grp"), P(("grp", "dev"), None)),
        check_vma=False,
    )
```

```python
import jax
import jax.numpy as jnp
from jax import lax
from jax.experimental import pallas as pl
from jax.experimental.pallas import tpu as pltpu
from jax.sharding import PartitionSpec as P

D = 8192
TOKENS = 3584
PANEL = 128
DAMPING = 0.01
MESH = pl.DeviceIdType.MESH
F32, BF16 = jnp.float32, jnp.bfloat16
HIGHEST = lax.Precision.HIGHEST

N_COPIES = 176


def dot(a, b, dims, precision=None):
    return lax.dot_general(a, b, (dims, ((), ())), precision=precision, preferred_element_type=F32)


def rel(i, o):
    return lax.rem(i + o, 4)


def kernel(
    a_hbm, c_hbm, q_hbm, v_hbm, f_hbm, p_hbm, upd_ref, new_ref,
    q, f, v, act, rot, cot, pan, scale, moment,
    send_c, recv_c, out2, recv2, out1p, out1m, recv1m, recv1p, out_z, recv_z, total, s, acc,
    im_part, im_c, im_s, im_x, im_xs, im_z,
    gr, gr_c, gr_h, gr_x, gr_q, gr_l, gr_l2, gr_y, gr_y2, gr_z, gr_full, chol,
    send_sem, recv_sem, local_sem,
):
    grp, dev = lax.axis_index("grp"), lax.axis_index("dev")
    y, h = grp // 4, lax.rem(grp, 4)
    c = lax.rem(dev, 2)
    x = lax.rem(dev // 2, 4)
    z = dev // 8
    other = 1 - c

    def at(yy=y, hh=h, zz=z, xx=x, cc=c):
        return (yy * 4 + hh, (zz * 4 + xx) * 2 + cc)

    core_peer = at(cc=other)
    x_peer = {o: at(xx=rel(x, o)) for o in (1, 2, 3)}
    z_peer = {o: at(zz=rel(z, o)) for o in (1, 2, 3)}
    y_peer = {o: at(yy=rel(y, o)) for o in (1, 2, 3)}
    h_peer = {o: at(hh=rel(h, o)) for o in (1, 2, 3)}
    peers = [core_peer]
    for table in (x_peer, z_peer, y_peer, h_peer):
        peers += [table[o] for o in (1, 2, 3)]

    barrier = pltpu.get_barrier_semaphore()
    for peer in peers:
        pl.semaphore_signal(barrier, inc=1, device_id=peer, device_id_type=MESH)

    pairs = (
        (p_hbm, pan.at[h, y]), (c_hbm, cot.at[x, z, c]), (a_hbm, act), (q_hbm, q),
        (f_hbm, f), (v_hbm, v),
    )
    loads = [pltpu.make_async_copy(src, dst, local_sem.at[n]) for n, (src, dst) in enumerate(pairs)]
    for load in loads:
        load.start()
    for load in loads[:2]:
        load.wait()
    pl.semaphore_wait(barrier, len(peers))

    started, received = [], []

    def push(src, dst, peer):
        n = len(started)
        copy = pltpu.make_async_remote_copy(
            src_ref=src, dst_ref=dst, send_sem=send_sem.at[n], recv_sem=recv_sem.at[n],
            device_id=peer, device_id_type=MESH,
        )
        copy.start()
        started.append(copy)
        return copy

    def need(*copies):
        for copy in copies:
            assert id(copy) not in received
            received.append(id(copy))
            copy.wait_recv()

    cot_x, cot_z, cot_f, cot_c = {}, {}, {}, {}

    def cot_push(xx, zz, peer):
        return push(cot.at[xx, zz, c], cot.at[xx, zz, c], peer)

    def cot_forward(j):
        zz = rel(z, j)
        need(cot_x[1, j], cot_x[3, j])
        o = 1 if j < 2 else 3
        cot_f[j] = cot_push(rel(x, 4 - o), zz, x_peer[o])

    def cot_pair(o):
        part = cot.at[rel(x, o), :, c]
        cot_c[o] = push(part, part, core_peer)

    order = (2, 1, 3, 0)

    def columns(k, oz, ox, cc):
        start = ((rel(z, oz) * 4 + rel(x, ox)) * 2 + cc) * 256 + k * 128
        return q[:, pl.ds(pl.multiple_of(start, 128), 128)]

    def block(k, ox, j, cc):
        return dot(act[...], columns(k, order[j], ox, cc), ((1,), (0,)))

    core, far, plus, minus, near = {}, {}, {}, {}, {}

    def send_core(k):
        for ox in (2, 3, 1, 0):
            for j in range(4):
                send_c[k, ox, j] = block(k, ox, j, other).astype(BF16)
            core[k, ox] = push(send_c.at[k, ox], recv_c.at[k, ox], core_peer)

    def pair_sum(k, ox, j):
        return block(k, ox, j, c) + recv_c[k, ox, j].astype(F32)

    def send_far(k, j):
        out2[k, j] = pair_sum(k, 2, j).astype(BF16)
        far[k, j] = push(out2.at[k, j], recv2.at[k, j], x_peer[1 if j < 2 else 3])

    def send_plus(k, j):
        total_j = pair_sum(k, 1, j)
        if j < 2:
            need(far[k, j])
            total_j = total_j + recv2[k, j].astype(F32)
        out1p[k, j] = total_j.astype(BF16)
        plus[k, j] = push(out1p.at[k, j], recv1m.at[k, j], x_peer[1])

    def send_minus(k, j):
        total_j = pair_sum(k, 3, j)
        if j >= 2:
            need(far[k, j])
            total_j = total_j + recv2[k, j].astype(F32)
        out1m[k, j] = total_j.astype(BF16)
        minus[k, j] = push(out1m.at[k, j], recv1p.at[k, j], x_peer[3])

    def send_first(k):
        need(core[k, 2])
        for j in (0, 2, 1, 3):
            send_far(k, j)
        need(core[k, 3])
        send_minus(k, 0)
        send_minus(k, 1)
        need(core[k, 1])
        send_plus(k, 2)
        send_plus(k, 3)

    def send_second(k):
        send_plus(k, 0)
        send_minus(k, 2)
        send_plus(k, 1)
        send_minus(k, 3)

    def send_z(k):
        need(core[k, 0])
        for j in range(4):
            total_j = pair_sum(k, 0, j)
            need(plus[k, j], minus[k, j])
            total_j = total_j + recv1m[k, j].astype(F32) + recv1p[k, j].astype(F32)
            if order[j]:
                out_z[k, j] = total_j.astype(BF16)
                near[k, j] = push(out_z.at[k, j], recv_z.at[k, j], z_peer[order[j]])
            else:
                total[k] = total_j

    rot_h, rot_hf, rot_y = {}, {}, {}

    def rot_to_y(k, j):
        block_j = rot.at[k, rel(h, j), y]
        for o in (2, 1, 3):
            rot_y[k, o, j] = push(block_j, block_j, y_peer[o])

    def rot_own(k):
        sum_k = total[k]
        for j in range(3):
            need(near[k, j])
            sum_k = sum_k + recv_z[k, j].astype(F32)
        rot[k, h, y] = sum_k.astype(BF16)
        for o in (1, 3):
            rot_h[k, o] = push(rot.at[k, h, y], rot.at[k, h, y], h_peer[o])
        rot_to_y(k, 0)

    def rot_next(k):
        for o in (1, 3):
            need(rot_h[k, o])
            lo = 0 if o == 1 else 112
            part = rot.at[k, rel(h, 4 - o), y, lo : lo + 112]
            rot_hf[k, o] = push(part, part, h_peer[o])
            rot_to_y(k, 4 - o)

    def rot_last(k):
        need(rot_hf[k, 1], rot_hf[k, 3])
        rot_to_y(k, 2)

    def add_tokens(k, j):
        need(rot_y[k, 1, j], rot_y[k, 2, j], rot_y[k, 3, j])
        hh = rel(h, j)
        part = dot(rot[k, hh].reshape(896, 128), cot[hh].reshape(896, 256), ((0,), (0,)))
        if j == 0:
            moment[k] = part
        else:
            moment[k] += part

    s_z, s_x, s_f, s_c = {}, {}, {}, {}

    def gather_own(k):
        s[k, 0, 0, c] = (moment[k] * scale[k * 128 : (k + 1) * 128, :]).astype(BF16)
        mine = s.at[k, 0, 0, c]
        for o in (2, 1, 3):
            s_z[k, o] = push(mine, s.at[k, 0, 4 - o, c], z_peer[o])
        for o in (1, 3):
            s_x[k, o, 0] = push(mine, s.at[k, 4 - o, 0, c], x_peer[o])

    def gather_z(k, o):
        need(s_z[k, o])
        j = 4 - o
        for ox in (1, 3):
            s_x[k, ox, j] = push(s.at[k, 0, j, c], s.at[k, 4 - ox, j, c], x_peer[ox])

    def gather_pair(k, ox, lo, hi):
        part = s.at[k, ox, lo:hi, c]
        s_c[k, ox, lo] = push(part, part, core_peer)

    def gather_forward(k, j):
        need(s_x[k, 1, j], s_x[k, 3, j])
        o = 1 if j < 2 else 3
        s_f[k, j] = push(s.at[k, 4 - o, j, c], s.at[k, 2, j, c], x_peer[o])

    def add_blocks(k, ox, lo, hi):
        need(s_c[k, ox, lo])
        sum_j = jnp.zeros((256, 256), F32)
        for j in range(lo, hi):
            for cc in (0, 1):
                sum_j = sum_j + dot(columns(k, j, ox, cc), s[k, ox, j, cc], ((1,), (0,)))
        if k == 0 and ox == 0:
            acc[...] = sum_j
        else:
            acc[...] += sum_j

    lane = lax.broadcasted_iota(jnp.int32, (8, PANEL), 1)
    row = lax.broadcasted_iota(jnp.int32, (8, PANEL), 0)

    def eliminate(b):
        k0 = 8 * b
        r = chol[k0 : k0 + 8, :PANEL]
        w = chol[k0 : k0 + 8, PANEL:]
        for i in range(8):
            column = r[:, k0 + i : k0 + i + 1]
            pivot = column[i : i + 1, :]
            inv = lax.rsqrt(pivot)
            inv = inv * (1.5 - 0.5 * pivot * inv * inv)
            below = column * inv
            r_row = r[i : i + 1, :] * inv
            w_row = w[i : i + 1, :] * inv
            r = jnp.where(row == i, r_row, jnp.where(row > i, r - below * r_row, r))
            w = jnp.where(row == i, w_row, jnp.where(row > i, w - below * w_row, w))
        if b < 15:
            r = jnp.where(lane >= k0 + 8, r, 0.0)
            chol[...] -= dot(r, jnp.concatenate([r, w], axis=1), ((0,), (0,)), HIGHEST)
        chol[k0 : k0 + 8, PANEL:] = w

    def panel_y():
        need(*pan_h.values())
        return {o: push(pan.at[:, y], pan.at[:, y], y_peer[o]) for o in (2, 1, 3)}

    def image_core():
        need(*pan_y.values())
        loads[4].wait()
        pan_t = pan[...].transpose(1, 0, 2, 3).reshape(PANEL, 256)
        im_part[...] = dot(f[...], pan_t, ((1,), (1,)), HIGHEST).reshape(4, 4, 2, 16, PANEL)
        return push(im_part.at[:, :, other], im_c, core_peer)

    def image_x():
        need(im_core)
        im_s[...] = im_part[:, :, c] + im_c[...]
        return {o: push(im_s.at[:, rel(x, o)], im_x.at[o], x_peer[o]) for o in (1, 2, 3)}

    def image_z():
        need(*im_xc.values())
        im_xs[...] = im_s[:, x] + im_x[1] + im_x[2] + im_x[3]
        return {o: push(im_xs.at[rel(z, o)], im_z.at[o], z_peer[o]) for o in (1, 2, 3)}

    def gram_core():
        need(*im_zc.values())
        image = im_xs[z] + im_z[1] + im_z[2] + im_z[3]
        gr[...] = dot(image, image, ((0,), (0,)), HIGHEST) * (1.0 / D)
        chol[:, PANEL:] = jnp.concatenate([image, jnp.zeros((PANEL - 16, PANEL), F32)], axis=0).T
        return push(gr.at[pl.ds(pl.multiple_of(other * 64, 64), 64)], gr_c, core_peer)

    def gram_x():
        need(gr_core)
        gr_h[...] = gr[pl.ds(pl.multiple_of(c * 64, 64), 64), :] + gr_c[...]
        return {
            o: push(
                gr_h.at[pl.ds(pl.multiple_of(rel(x, o) * 16, 16), 16)], gr_x.at[o], x_peer[o]
            )
            for o in (1, 2, 3)
        }

    def gram_z():
        need(*gr_xc.values())
        mine = gr_h[pl.ds(pl.multiple_of(x * 16, 16), 16), :]
        gr_q[...] = mine + gr_x[1] + gr_x[2] + gr_x[3]
        return {o: push(gr_q, gr_l.at[o], z_peer[o]) for o in (1, 2, 3)}

    def gram_y():
        need(*gr_zc.values())
        gr_l2[...] = gr_q[...] + gr_l[1] + gr_l[2] + gr_l[3]
        return {o: push(gr_l2, gr_y.at[o], y_peer[o]) for o in (1, 2, 3)}

    def gram_h():
        need(*gr_yc.values())
        gr_y2[...] = gr_l2[...] + gr_y[1] + gr_y[2] + gr_y[3]
        return {o: push(gr_y2, gr_z.at[o], h_peer[o]) for o in (1, 2, 3)}

    def gram_x_back():
        need(*gr_hc.values())
        lo = pl.ds(pl.multiple_of(c * 64 + x * 16, 16), 16)
        gr_full[lo, :] = gr_y2[...] + gr_z[1] + gr_z[2] + gr_z[3]
        return {o: push(gr_full.at[lo], gr_full.at[lo], x_peer[o]) for o in (1, 2, 3)}

    def gram_core_back():
        need(*gr_xg.values())
        half = pl.ds(pl.multiple_of(c * 64, 64), 64)
        return push(gr_full.at[half], gr_full.at[half], core_peer)

    pan_h = {o: push(pan.at[h, y], pan.at[h, y], h_peer[o]) for o in (2, 1, 3)}
    for o in (2, 1, 3):
        cot_z[o] = cot_push(x, z, z_peer[o])
    loads[2].wait()
    loads[3].wait()
    send_core(0)
    send_first(0)
    send_core(1)
    loads[5].wait()
    scale[...] = (1.0 / TOKENS) / (v[...].astype(F32) + DAMPING)
    send_second(0)
    pan_y = panel_y()
    send_first(1)
    im_core = image_core()
    send_z(0)
    im_xc = image_x()
    send_second(1)
    for o in (1, 3):
        cot_x[o, 0] = cot_push(x, z, x_peer[o])
    for o in (1, 3, 2):
        need(cot_z[o])
        for ox in (1, 3):
            cot_x[ox, 4 - o] = cot_push(x, rel(z, 4 - o), x_peer[ox])
    cot_pair(0)
    im_zc = image_z()
    rot_own(0)
    send_z(1)
    gr_core = gram_core()
    for j in (0, 3, 1, 2):
        cot_forward(j)
    cot_pair(1)
    cot_pair(3)
    gr_xc = gram_x()
    rot_next(0)
    rot_own(1)
    need(*cot_f.values())
    cot_pair(2)
    gr_zc = gram_z()
    rot_last(0)
    rot_next(1)
    gr_yc = gram_y()
    need(*cot_c.values())
    for j in (0, 3, 1, 2):
        add_tokens(0, j)
    gather_own(0)
    rot_last(1)
    gr_hc = gram_h()
    gather_z(0, 1)
    gather_z(0, 3)
    gather_z(0, 2)
    gather_pair(0, 0, 0, 4)
    for j in (0, 3, 1, 2):
        add_tokens(1, j)
    gather_own(1)
    gr_xg = gram_x_back()
    gather_forward(0, 0)
    gather_forward(0, 3)
    gr_cg = gram_core_back()
    gather_forward(0, 1)
    gather_forward(0, 2)
    gather_pair(0, 1, 0, 4)
    gather_pair(0, 3, 0, 4)
    need(gr_cg)
    chol[:, :PANEL] = gr_full[...]
    steps = iter(range(16))
    add_blocks(0, 0, 0, 4)
    eliminate(next(steps))
    for o in (1, 3, 2):
        gather_z(1, o)
        eliminate(next(steps))
    gather_pair(1, 0, 0, 4)
    add_blocks(0, 1, 0, 4)
    add_blocks(0, 3, 0, 4)
    need(s_f[0, 0], s_f[0, 1])
    gather_pair(0, 2, 0, 2)
    need(s_f[0, 2], s_f[0, 3])
    gather_pair(0, 2, 2, 4)
    for j in (0, 3, 1, 2):
        eliminate(next(steps))
        gather_forward(1, j)
    gather_pair(1, 1, 0, 4)
    gather_pair(1, 3, 0, 4)
    add_blocks(0, 2, 0, 2)
    add_blocks(0, 2, 2, 4)
    add_blocks(1, 0, 0, 4)
    for b in steps:
        eliminate(b)
    need(s_f[1, 0], s_f[1, 1])
    gather_pair(1, 2, 0, 2)
    need(s_f[1, 2], s_f[1, 3])
    gather_pair(1, 2, 2, 4)
    new_ref[...] = chol[:, PANEL:].T[:16, :]
    add_blocks(1, 1, 0, 4)
    add_blocks(1, 3, 0, 4)
    add_blocks(1, 2, 0, 2)
    add_blocks(1, 2, 2, 4)
    upd_ref[...] = acc[...].astype(BF16)
    for copy in started:
        copy.wait_send()
    assert len(started) <= N_COPIES
    assert len(started) == len(received)


def body(activations, cotangent, eigenbasis, second_moment, factor, old_panel):
    vmem = pl.BlockSpec(memory_space=pltpu.VMEM)
    hbm = pl.BlockSpec(memory_space=pl.ANY)
    tile = (224, 128)
    half = (128, 256)
    part = (16, PANEL)
    scratch = [
        pltpu.VMEM((256, D), BF16),
        pltpu.VMEM((512, 256), F32),
        pltpu.VMEM((256, 256), BF16),
        pltpu.VMEM((224, 256), BF16),
        pltpu.VMEM((2, 4, 4) + tile, BF16),
        pltpu.VMEM((4, 4, 2, 112, 256), BF16),
        pltpu.VMEM((4, 4, 8, 256), F32),
        pltpu.VMEM((256, 256), F32),
        pltpu.VMEM((2,) + half, F32),
        pltpu.VMEM((2, 4, 4) + tile, BF16),
        pltpu.VMEM((2, 4, 4) + tile, BF16),
        pltpu.VMEM((2, 4) + tile, BF16),
        pltpu.VMEM((2, 4) + tile, BF16),
        pltpu.VMEM((2, 4) + tile, BF16),
        pltpu.VMEM((2, 4) + tile, BF16),
        pltpu.VMEM((2, 4) + tile, BF16),
        pltpu.VMEM((2, 4) + tile, BF16),
        pltpu.VMEM((2, 3) + tile, BF16),
        pltpu.VMEM((2, 3) + tile, BF16),
        pltpu.VMEM((2,) + tile, F32),
        pltpu.VMEM((2, 4, 4, 2) + half, BF16),
        pltpu.VMEM((256, 256), F32),
        pltpu.VMEM((4, 4, 2) + part, F32),
        pltpu.VMEM((4, 4) + part, F32),
        pltpu.VMEM((4, 4) + part, F32),
        pltpu.VMEM((4, 4) + part, F32),
        pltpu.VMEM((4,) + part, F32),
        pltpu.VMEM((4,) + part, F32),
        pltpu.VMEM((PANEL, PANEL), F32),
        pltpu.VMEM((64, PANEL), F32),
        pltpu.VMEM((64, PANEL), F32),
        pltpu.VMEM((4,) + part, F32),
        pltpu.VMEM(part, F32),
        pltpu.VMEM((4,) + part, F32),
        pltpu.VMEM(part, F32),
        pltpu.VMEM((4,) + part, F32),
        pltpu.VMEM(part, F32),
        pltpu.VMEM((4,) + part, F32),
        pltpu.VMEM((PANEL, PANEL), F32),
        pltpu.VMEM((PANEL, 2 * PANEL), F32),
        pltpu.SemaphoreType.DMA((N_COPIES,)),
        pltpu.SemaphoreType.DMA((N_COPIES,)),
        pltpu.SemaphoreType.DMA((6,)),
    ]
    return pl.pallas_call(
        kernel,
        out_shape=(
            jax.ShapeDtypeStruct((256, 256), BF16),
            jax.ShapeDtypeStruct(part, F32),
        ),
        in_specs=[hbm] * 6,
        out_specs=(vmem, vmem),
        scratch_shapes=scratch,
        compiler_params=pltpu.CompilerParams(
            collective_id=0, has_side_effects=True, vmem_limit_bytes=60 * 1024 * 1024
        ),
    )(
        activations, cotangent, eigenbasis, second_moment, factor, old_panel.T
    )


def solution(mesh):
    return jax.shard_map(
        body,
        mesh=mesh,
        in_specs=(
            P("grp", "dev"),
            P("dev", "grp"),
            P("dev", None),
            P("dev", "grp"),
            P("grp", "dev"),
            P("dev", "grp"),
        ),
        out_specs=(P("dev", "grp"), P(("grp", "dev"), None)),
        check_vma=False,
    )
```

```python
import math

import jax
import jax.numpy as jnp
from jax import lax
from jax.experimental import pallas as pl
from jax.experimental.pallas import tpu as pltpu
from jax.sharding import PartitionSpec as P

D = 8192
TOKENS = 3584
PANEL = 128
DAMPING = 0.01
MESH = pl.DeviceIdType.MESH
F32, BF16 = jnp.float32, jnp.bfloat16
HIGHEST = lax.Precision.HIGHEST

N_SENT = 32
N_RECEIVED = 92


def dot(a, b, dims, precision=None):
    return lax.dot_general(a, b, (dims, ((), ())), precision=precision, preferred_element_type=F32)


def rel(i, o):
    return lax.rem(i + o, 4)


def kernel(
    a_hbm, c_hbm, q_hbm, v_hbm, f_hbm, p_hbm, upd_ref, new_ref,
    q, f, v, act, rot, cot, pan, scale, moment,
    send_c, recv_c, out2, recv2, out1p, out1m, recv1m, recv1p, out_z, recv_z, total, s, acc,
    im_part, im_c, im_s, im_x, im_xs, im_z,
    gr, gr_c, gr_h, gr_x, gr_q, gr_l, gr_l2, gr_y, gr_y2, gr_z, gr_full, chol,
    send_sem, recv_sem, local_sem,
):
    grp, dev = lax.axis_index("grp"), lax.axis_index("dev")
    y, h = grp // 4, lax.rem(grp, 4)
    c = lax.rem(dev, 2)
    x = lax.rem(dev // 2, 4)
    z = dev // 8
    other = 1 - c

    def at(yy=y, hh=h, zz=z, xx=x, cc=c):
        return (yy * 4 + hh, (zz * 4 + xx) * 2 + cc)

    core_peer = at(cc=other)
    x_peer = {o: at(xx=rel(x, o)) for o in (1, 2, 3)}
    z_peer = {o: at(zz=rel(z, o)) for o in (1, 2, 3)}
    y_peer = {o: at(yy=rel(y, o)) for o in (1, 2, 3)}
    h_peer = {o: at(hh=rel(h, o)) for o in (1, 2, 3)}
    peers = [core_peer]
    for table in (x_peer, z_peer, y_peer, h_peer):
        peers += [table[o] for o in (1, 2, 3)]

    barrier = pltpu.get_barrier_semaphore()
    for peer in peers:
        pl.semaphore_signal(barrier, inc=1, device_id=peer, device_id_type=MESH)

    pairs = (
        (p_hbm, pan.at[h, y]), (c_hbm, cot.at[x, z, c]), (a_hbm, act), (q_hbm, q),
        (f_hbm, f), (v_hbm, v),
    )
    loads = [pltpu.make_async_copy(src, dst, local_sem.at[n]) for n, (src, dst) in enumerate(pairs)]
    for load in loads:
        load.start()
    for load in loads[:2]:
        load.wait()
    pl.semaphore_wait(barrier, len(peers))

    sent, received = {}, {}

    def push(group, key, src, dst, peer):
        copy = pltpu.make_async_remote_copy(
            src_ref=src, dst_ref=dst,
            send_sem=send_sem.at[sent.setdefault(group, [len(sent), 0])[0]],
            recv_sem=recv_sem.at[received.setdefault((group, key), [len(received), 0])[0]],
            device_id=peer, device_id_type=MESH,
        )
        copy.start()
        size = math.prod(src.shape) * src.dtype.itemsize
        sent[group][1] += size
        received[group, key][1] += size

    def wait_bytes(semaphore, entry, like):
        assert entry[1] == math.prod(like.shape) * like.dtype.itemsize
        entry[1] = 0
        pltpu.make_async_copy(like, like, semaphore.at[entry[0]]).wait()

    def need(group, key, like):
        wait_bytes(recv_sem, received[group, key], like)

    def cot_push(group, key, xx, zz, peer):
        push(group, key, cot.at[xx, zz, c], cot.at[xx, zz, c], peer)

    def cot_forward(j):
        need("cot_x", j, cot.at[0, 0:2, 0])
        o = 1 if j < 2 else 3
        cot_push("cot_f", 0, rel(x, 4 - o), rel(z, j), x_peer[o])

    def cot_pair(o):
        part = cot.at[rel(x, o), :, c]
        push("cot_c", 0, part, part, core_peer)

    order = (2, 1, 3, 0)

    def columns(k, oz, ox, cc):
        start = ((rel(z, oz) * 4 + rel(x, ox)) * 2 + cc) * 256 + k * 128
        return q[:, pl.ds(pl.multiple_of(start, 128), 128)]

    def block(k, ox, j, cc):
        return dot(act[...], columns(k, order[j], ox, cc), ((1,), (0,)))

    def send_core(k):
        for ox in (2, 3, 1, 0):
            for j in range(4):
                send_c[k, ox, j] = block(k, ox, j, other).astype(BF16)
            push("core", (k, ox), send_c.at[k, ox], recv_c.at[k, ox], core_peer)

    def pair_sum(k, ox, j):
        return block(k, ox, j, c) + recv_c[k, ox, j].astype(F32)

    def send_far(k, j):
        out2[k, j] = pair_sum(k, 2, j).astype(BF16)
        push("far", (k, j), out2.at[k, j], recv2.at[k, j], x_peer[1 if j < 2 else 3])

    def send_plus(k, j):
        total_j = pair_sum(k, 1, j)
        if j < 2:
            need("far", (k, j), recv2.at[k, j])
            total_j = total_j + recv2[k, j].astype(F32)
        out1p[k, j] = total_j.astype(BF16)
        push("near_x", (k, j), out1p.at[k, j], recv1m.at[k, j], x_peer[1])

    def send_minus(k, j):
        total_j = pair_sum(k, 3, j)
        if j >= 2:
            need("far", (k, j), recv2.at[k, j])
            total_j = total_j + recv2[k, j].astype(F32)
        out1m[k, j] = total_j.astype(BF16)
        push("near_x", (k, j), out1m.at[k, j], recv1p.at[k, j], x_peer[3])

    def send_first(k):
        need("core", (k, 2), recv_c.at[k, 2])
        for j in (0, 2, 1, 3):
            send_far(k, j)
        need("core", (k, 3), recv_c.at[k, 3])
        send_minus(k, 0)
        send_minus(k, 1)
        need("core", (k, 1), recv_c.at[k, 1])
        send_plus(k, 2)
        send_plus(k, 3)

    def send_second(k):
        send_plus(k, 0)
        send_minus(k, 2)
        send_plus(k, 1)
        send_minus(k, 3)

    def send_z(k):
        need("core", (k, 0), recv_c.at[k, 0])
        for j in range(4):
            total_j = pair_sum(k, 0, j)
            need("near_x", (k, j), recv1m.at[k, 0:2])
            total_j = total_j + recv1m[k, j].astype(F32) + recv1p[k, j].astype(F32)
            if order[j]:
                out_z[k, j] = total_j.astype(BF16)
                push("near_z", k, out_z.at[k, j], recv_z.at[k, j], z_peer[order[j]])
            else:
                total[k] = total_j

    def rot_to_y(k, j):
        block_j = rot.at[k, rel(h, j), y]
        for o in (2, 1, 3):
            push("rot_y", (k, j), block_j, block_j, y_peer[o])

    def rot_own(k):
        need("near_z", k, recv_z.at[k])
        sum_k = total[k]
        for j in range(3):
            sum_k = sum_k + recv_z[k, j].astype(F32)
        rot[k, h, y] = sum_k.astype(BF16)
        for o in (1, 3):
            push("rot_h", (k, o), rot.at[k, h, y], rot.at[k, h, y], h_peer[o])
        rot_to_y(k, 0)

    def rot_next(k):
        for o in (1, 3):
            need("rot_h", (k, o), rot.at[k, 0, 0])
            lo = 0 if o == 1 else 112
            part = rot.at[k, rel(h, 4 - o), y, lo : lo + 112]
            push("rot_h", (k, 2), part, part, h_peer[o])
            rot_to_y(k, 4 - o)

    def rot_last(k):
        need("rot_h", (k, 2), rot.at[k, 0, 0])
        rot_to_y(k, 2)

    def add_tokens(k, j):
        need("rot_y", (k, j), rot.at[k, 0, 0:3])
        hh = rel(h, j)
        part = dot(rot[k, hh].reshape(896, 128), cot[hh].reshape(896, 256), ((0,), (0,)))
        if j == 0:
            moment[k] = part
        else:
            moment[k] += part

    def gather_own(k):
        s[k, 0, 0, c] = (moment[k] * scale[k * 128 : (k + 1) * 128, :]).astype(BF16)
        mine = s.at[k, 0, 0, c]
        for o in (2, 1, 3):
            push("s_z", (k, o), mine, s.at[k, 0, 4 - o, c], z_peer[o])
        for o in (1, 3):
            push("s_x", (k, 0), mine, s.at[k, 4 - o, 0, c], x_peer[o])

    def gather_z(k, o):
        need("s_z", (k, o), s.at[k, 0, 0, 0])
        j = 4 - o
        for ox in (1, 3):
            push("s_x", (k, j), s.at[k, 0, j, c], s.at[k, 4 - ox, j, c], x_peer[ox])

    def gather_pair(k, ox, lo, hi):
        part = s.at[k, ox, lo:hi, c]
        push("s_c", (k, ox, lo), part, part, core_peer)

    def gather_forward(k, j):
        need("s_x", (k, j), s.at[k, 0, 0:2, 0])
        o = 1 if j < 2 else 3
        push("s_f", (k, j // 2), s.at[k, 4 - o, j, c], s.at[k, 2, j, c], x_peer[o])

    def add_blocks(k, ox, lo, hi):
        need("s_c", (k, ox, lo), s.at[k, 0, 0 : hi - lo, 0])
        sum_j = jnp.zeros((256, 256), F32)
        for j in range(lo, hi):
            for cc in (0, 1):
                sum_j = sum_j + dot(columns(k, j, ox, cc), s[k, ox, j, cc], ((1,), (0,)))
        if k == 0 and ox == 0:
            acc[...] = sum_j
        else:
            acc[...] += sum_j

    lane = lax.broadcasted_iota(jnp.int32, (16, 2 * PANEL), 1)
    row = lax.broadcasted_iota(jnp.int32, (16, 2 * PANEL), 0)

    def eliminate(b):
        k0 = 16 * b
        r = chol[k0 : k0 + 16, :]
        for i in range(16):
            column = r[:, k0 + i : k0 + i + 1]
            pivot = column[i : i + 1, :]
            inv = lax.rsqrt(pivot)
            inv = inv * (1.5 - 0.5 * pivot * inv * inv)
            below = column * inv
            r_row = r[i : i + 1, :] * inv
            r = jnp.where(row == i, r_row, jnp.where(row > i, r - below * r_row, r))
        chol[k0 : k0 + 16, :] = r
        if b < 7:
            r = jnp.where(lane >= k0 + 16, r, 0.0)
            hi = r.astype(BF16)
            rest = r - hi.astype(F32)
            mid = rest.astype(BF16)
            low = (rest - mid.astype(F32)).astype(BF16)
            left = jnp.concatenate([hi, hi, hi, mid, mid, low], axis=0)[:, :PANEL]
            right = jnp.concatenate([hi, mid, low, hi, mid, hi], axis=0)
            chol[k0 + 16 :, :] -= dot(left, right, ((0,), (0,)))[k0 + 16 :, :]

    def panel_y():
        need("pan_h", 0, pan.at[0, 0:3])
        for o in (1, 2, 3):
            push("pan_y", 0, pan.at[:, y], pan.at[:, y], y_peer[o])

    def image_core():
        need("pan_y", 0, pan.at[0:3])
        loads[4].wait()
        pan_t = pan[...].transpose(1, 0, 2, 3).reshape(PANEL, 256)
        im_part[...] = dot(f[...], pan_t, ((1,), (1,)), HIGHEST).reshape(4, 4, 2, 16, PANEL)
        push("im_core", 0, im_part.at[:, :, other], im_c, core_peer)

    def image_x():
        need("im_core", 0, im_c)
        im_s[...] = im_part[:, :, c] + im_c[...]
        for o in (1, 2, 3):
            push("im_xc", 0, im_s.at[:, rel(x, o)], im_x.at[o], x_peer[o])

    def image_z():
        need("im_xc", 0, im_x.at[1:4])
        im_xs[...] = im_s[:, x] + im_x[1] + im_x[2] + im_x[3]
        for o in (1, 2, 3):
            push("im_zc", 0, im_xs.at[rel(z, o)], im_z.at[o], z_peer[o])

    def gram_core():
        need("im_zc", 0, im_z.at[1:4])
        image = im_xs[z] + im_z[1] + im_z[2] + im_z[3]
        gr[...] = dot(image, image, ((0,), (0,)), HIGHEST) * (1.0 / D)
        chol[:, PANEL:] = jnp.concatenate([image, jnp.zeros((PANEL - 16, PANEL), F32)], axis=0).T
        push("gr_core", 0, gr.at[pl.ds(pl.multiple_of(other * 64, 64), 64)], gr_c, core_peer)

    def gram_x():
        need("gr_core", 0, gr_c)
        gr_h[...] = gr[pl.ds(pl.multiple_of(c * 64, 64), 64), :] + gr_c[...]
        for o in (1, 2, 3):
            share = pl.ds(pl.multiple_of(rel(x, o) * 16, 16), 16)
            push("gr_xc", 0, gr_h.at[share], gr_x.at[o], x_peer[o])

    def gram_z():
        need("gr_xc", 0, gr_x.at[1:4])
        mine = gr_h[pl.ds(pl.multiple_of(x * 16, 16), 16), :]
        gr_q[...] = mine + gr_x[1] + gr_x[2] + gr_x[3]
        for o in (1, 2, 3):
            push("gr_zc", 0, gr_q, gr_l.at[o], z_peer[o])

    def gram_y():
        need("gr_zc", 0, gr_l.at[1:4])
        gr_l2[...] = gr_q[...] + gr_l[1] + gr_l[2] + gr_l[3]
        for o in (1, 2, 3):
            push("gr_yc", 0, gr_l2, gr_y.at[o], y_peer[o])

    def gram_h():
        need("gr_yc", 0, gr_y.at[1:4])
        gr_y2[...] = gr_l2[...] + gr_y[1] + gr_y[2] + gr_y[3]
        for o in (1, 2, 3):
            push("gr_hc", 0, gr_y2, gr_z.at[o], h_peer[o])

    def gram_x_back():
        need("gr_hc", 0, gr_z.at[1:4])
        lo = pl.ds(pl.multiple_of(c * 64 + x * 16, 16), 16)
        gr_full[lo, :] = gr_y2[...] + gr_z[1] + gr_z[2] + gr_z[3]
        for o in (1, 2, 3):
            push("gr_xg", 0, gr_full.at[lo], gr_full.at[lo], x_peer[o])

    def gram_core_back():
        need("gr_xg", 0, gr_full.at[0:48])
        half = pl.ds(pl.multiple_of(c * 64, 64), 64)
        push("gr_cg", 0, gr_full.at[half], gr_full.at[half], core_peer)

    for o in (2, 1, 3):
        push("pan_h", 0, pan.at[h, y], pan.at[h, y], h_peer[o])
    for o in (2, 1, 3):
        cot_push("cot_z", o, x, z, z_peer[o])
    loads[2].wait()
    loads[3].wait()
    send_core(0)
    send_first(0)
    send_core(1)
    loads[5].wait()
    scale[...] = (1.0 / TOKENS) / (v[...].astype(F32) + DAMPING)
    panel_y()
    send_second(0)
    send_first(1)
    image_core()
    send_z(0)
    image_x()
    send_second(1)
    for o in (1, 3):
        cot_push("cot_x", 0, x, z, x_peer[o])
    for o in (1, 3, 2):
        need("cot_z", o, cot.at[0, 0, 0])
        for ox in (1, 3):
            cot_push("cot_x", 4 - o, x, rel(z, 4 - o), x_peer[ox])
    cot_pair(0)
    image_z()
    rot_own(0)
    gram_core()
    send_z(1)
    gram_x()
    for j in (0, 3, 1, 2):
        cot_forward(j)
    cot_pair(1)
    cot_pair(3)
    gram_z()
    rot_next(0)
    gram_y()
    rot_own(1)
    need("cot_f", 0, cot.at[:, 0, 0])
    cot_pair(2)
    gram_h()
    rot_last(0)
    need("cot_c", 0, cot.at[:, :, 0])
    rot_next(1)
    for j in (0, 3, 1, 2):
        add_tokens(0, j)
    gather_own(0)
    gram_x_back()
    rot_last(1)
    gather_z(0, 1)
    gather_z(0, 3)
    gram_core_back()
    gather_z(0, 2)
    gather_pair(0, 0, 0, 4)
    need("gr_cg", 0, gr_full.at[0:64])
    chol[:, :PANEL] = gr_full[...]
    eliminate(0)
    for j in (0, 3, 1, 2):
        add_tokens(1, j)
    gather_own(1)
    gather_forward(0, 0)
    gather_forward(0, 3)
    eliminate(1)
    gather_forward(0, 1)
    gather_forward(0, 2)
    gather_pair(0, 1, 0, 4)
    gather_pair(0, 3, 0, 4)
    eliminate(2)
    gather_z(1, 1)
    gather_z(1, 3)
    eliminate(3)
    gather_z(1, 2)
    gather_pair(1, 0, 0, 4)
    need("s_f", (0, 0), s.at[0, 0, 0:2, 0])
    gather_pair(0, 2, 0, 2)
    need("s_f", (0, 1), s.at[0, 0, 0:2, 0])
    gather_pair(0, 2, 2, 4)
    eliminate(4)
    gather_forward(1, 0)
    gather_forward(1, 3)
    add_blocks(0, 0, 0, 4)
    eliminate(5)
    gather_forward(1, 1)
    gather_forward(1, 2)
    gather_pair(1, 1, 0, 4)
    gather_pair(1, 3, 0, 4)
    add_blocks(0, 1, 0, 4)
    add_blocks(0, 3, 0, 4)
    add_blocks(0, 2, 0, 2)
    add_blocks(0, 2, 2, 4)
    add_blocks(1, 0, 0, 4)
    eliminate(6)
    need("s_f", (1, 0), s.at[1, 0, 0:2, 0])
    gather_pair(1, 2, 0, 2)
    need("s_f", (1, 1), s.at[1, 0, 0:2, 0])
    gather_pair(1, 2, 2, 4)
    eliminate(7)
    new_ref[...] = chol[:, PANEL:].T[:16, :]
    add_blocks(1, 1, 0, 4)
    add_blocks(1, 3, 0, 4)
    add_blocks(1, 2, 0, 2)
    add_blocks(1, 2, 2, 4)
    upd_ref[...] = acc[...].astype(BF16)
    bytes_like = {
        "pan_h": pan.at[0, 0:3], "pan_y": pan.at[0:3], "im_core": im_c, "im_xc": im_x.at[1:4],
        "im_zc": im_z.at[1:4], "gr_core": gr_c, "gr_xc": gr_x.at[1:4], "gr_zc": gr_l.at[1:4],
        "gr_yc": gr_y.at[1:4], "gr_hc": gr_z.at[1:4], "gr_xg": gr_full.at[0:48],
        "gr_cg": gr_full.at[0:64], "cot_z": cot.at[0, 0:3, 0], "cot_x": cot.at[:, 0:2, 0],
        "cot_f": cot.at[:, 0, 0], "cot_c": cot.at[:, :, 0], "core": send_c, "far": out2,
        "near_x": send_c.at[:, 0:2], "near_z": out_z, "rot_h": rot.at[:, 0, 0:3],
        "rot_y": rot.at[:, 0:3], "s_z": s.at[:, 0, 0:3, 0], "s_x": s.at[:, 0:2, :, 0],
        "s_f": s.at[:, 0, :, 0], "s_c": s.at[:, :, :, 0],
    }
    for group, entry in sent.items():
        wait_bytes(send_sem, entry, bytes_like[group])
    assert len(sent) <= N_SENT and len(received) <= N_RECEIVED
    assert not any(size for _, size in received.values())


def body(activations, cotangent, eigenbasis, second_moment, factor, old_panel):
    vmem = pl.BlockSpec(memory_space=pltpu.VMEM)
    hbm = pl.BlockSpec(memory_space=pl.ANY)
    tile = (224, 128)
    half = (128, 256)
    part = (16, PANEL)
    scratch = [
        pltpu.VMEM((256, D), BF16),
        pltpu.VMEM((512, 256), F32),
        pltpu.VMEM((256, 256), BF16),
        pltpu.VMEM((224, 256), BF16),
        pltpu.VMEM((2, 4, 4) + tile, BF16),
        pltpu.VMEM((4, 4, 2, 112, 256), BF16),
        pltpu.VMEM((4, 4, 8, 256), F32),
        pltpu.VMEM((256, 256), F32),
        pltpu.VMEM((2,) + half, F32),
        pltpu.VMEM((2, 4, 4) + tile, BF16),
        pltpu.VMEM((2, 4, 4) + tile, BF16),
        pltpu.VMEM((2, 4) + tile, BF16),
        pltpu.VMEM((2, 4) + tile, BF16),
        pltpu.VMEM((2, 4) + tile, BF16),
        pltpu.VMEM((2, 4) + tile, BF16),
        pltpu.VMEM((2, 4) + tile, BF16),
        pltpu.VMEM((2, 4) + tile, BF16),
        pltpu.VMEM((2, 3) + tile, BF16),
        pltpu.VMEM((2, 3) + tile, BF16),
        pltpu.VMEM((2,) + tile, F32),
        pltpu.VMEM((2, 4, 4, 2) + half, BF16),
        pltpu.VMEM((256, 256), F32),
        pltpu.VMEM((4, 4, 2) + part, F32),
        pltpu.VMEM((4, 4) + part, F32),
        pltpu.VMEM((4, 4) + part, F32),
        pltpu.VMEM((4, 4) + part, F32),
        pltpu.VMEM((4,) + part, F32),
        pltpu.VMEM((4,) + part, F32),
        pltpu.VMEM((PANEL, PANEL), F32),
        pltpu.VMEM((64, PANEL), F32),
        pltpu.VMEM((64, PANEL), F32),
        pltpu.VMEM((4,) + part, F32),
        pltpu.VMEM(part, F32),
        pltpu.VMEM((4,) + part, F32),
        pltpu.VMEM(part, F32),
        pltpu.VMEM((4,) + part, F32),
        pltpu.VMEM(part, F32),
        pltpu.VMEM((4,) + part, F32),
        pltpu.VMEM((PANEL, PANEL), F32),
        pltpu.VMEM((PANEL, 2 * PANEL), F32),
        pltpu.SemaphoreType.DMA((N_SENT,)),
        pltpu.SemaphoreType.DMA((N_RECEIVED,)),
        pltpu.SemaphoreType.DMA((6,)),
    ]
    return pl.pallas_call(
        kernel,
        out_shape=(
            jax.ShapeDtypeStruct((256, 256), BF16),
            jax.ShapeDtypeStruct(part, F32),
        ),
        in_specs=[hbm] * 6,
        out_specs=(vmem, vmem),
        scratch_shapes=scratch,
        compiler_params=pltpu.CompilerParams(
            collective_id=0, has_side_effects=True, vmem_limit_bytes=60 * 1024 * 1024
        ),
    )(
        activations, cotangent, eigenbasis, second_moment, factor, old_panel.T
    )


def solution(mesh):
    return jax.shard_map(
        body,
        mesh=mesh,
        in_specs=(
            P("grp", "dev"),
            P("dev", "grp"),
            P("dev", None),
            P("dev", "grp"),
            P("grp", "dev"),
            P("dev", "grp"),
        ),
        out_specs=(P("dev", "grp"), P(("grp", "dev"), None)),
        check_vma=False,
    )
```

```python
import math

import jax
import jax.numpy as jnp
from jax import lax
from jax.experimental import pallas as pl
from jax.experimental.pallas import tpu as pltpu
from jax.sharding import PartitionSpec as P

D = 8192
TOKENS = 3584
PANEL = 128
DAMPING = 0.01
MESH = pl.DeviceIdType.MESH
F32, BF16 = jnp.float32, jnp.bfloat16
HIGHEST = lax.Precision.HIGHEST

N_SENT = 32
N_RECEIVED = 92


def dot(a, b, dims, precision=None):
    return lax.dot_general(a, b, (dims, ((), ())), precision=precision, preferred_element_type=F32)


def rel(i, o):
    return lax.rem(i + o, 4)


def kernel(
    a_hbm, c_hbm, q_hbm, v_hbm, f_hbm, p_hbm, upd_ref, new_ref,
    q, f, v, act, rot, cot, pan, scale, moment,
    send_c, recv_c, out2, recv2, out1p, out1m, recv1m, recv1p, out_z, recv_z, total, s, acc,
    im_part, im_c, im_s, im_x, im_xs, im_z,
    gr, gr_c, gr_h, gr_x, gr_q, gr_l, gr_l2, gr_y, gr_y2, gr_z, gr_full, chol,
    send_sem, recv_sem, local_sem,
):
    grp, dev = lax.axis_index("grp"), lax.axis_index("dev")
    y, h = grp // 4, lax.rem(grp, 4)
    c = lax.rem(dev, 2)
    x = lax.rem(dev // 2, 4)
    z = dev // 8
    other = 1 - c

    def at(yy=y, hh=h, zz=z, xx=x, cc=c):
        return (yy * 4 + hh, (zz * 4 + xx) * 2 + cc)

    core_peer = at(cc=other)
    x_peer = {o: at(xx=rel(x, o)) for o in (1, 2, 3)}
    z_peer = {o: at(zz=rel(z, o)) for o in (1, 2, 3)}
    y_peer = {o: at(yy=rel(y, o)) for o in (1, 2, 3)}
    h_peer = {o: at(hh=rel(h, o)) for o in (1, 2, 3)}
    peers = [core_peer]
    for table in (x_peer, z_peer, y_peer, h_peer):
        peers += [table[o] for o in (1, 2, 3)]

    barrier = pltpu.get_barrier_semaphore()
    for peer in peers:
        pl.semaphore_signal(barrier, inc=1, device_id=peer, device_id_type=MESH)

    pairs = (
        (p_hbm, pan.at[h, y]), (c_hbm, cot.at[x, z, c]), (a_hbm, act), (q_hbm, q),
        (f_hbm, f), (v_hbm, v),
    )
    loads = [pltpu.make_async_copy(src, dst, local_sem.at[n]) for n, (src, dst) in enumerate(pairs)]
    for load in loads:
        load.start()
    for load in loads[:2]:
        load.wait()
    pl.semaphore_wait(barrier, len(peers))

    sent, received = {}, {}

    def push(group, key, src, dst, peer):
        copy = pltpu.make_async_remote_copy(
            src_ref=src, dst_ref=dst,
            send_sem=send_sem.at[sent.setdefault(group, [len(sent), 0])[0]],
            recv_sem=recv_sem.at[received.setdefault((group, key), [len(received), 0])[0]],
            device_id=peer, device_id_type=MESH,
        )
        copy.start()
        size = math.prod(src.shape) * src.dtype.itemsize
        sent[group][1] += size
        received[group, key][1] += size

    def wait_bytes(semaphore, entry, like):
        assert entry[1] == math.prod(like.shape) * like.dtype.itemsize
        entry[1] = 0
        pltpu.make_async_copy(like, like, semaphore.at[entry[0]]).wait()

    def need(group, key, like):
        wait_bytes(recv_sem, received[group, key], like)

    def cot_push(group, key, xx, zz, peer):
        push(group, key, cot.at[xx, zz, c], cot.at[xx, zz, c], peer)

    def cot_forward(j):
        need("cot_x", j, cot.at[0, 0:2, 0])
        o = 1 if j < 2 else 3
        cot_push("cot_f", 0, rel(x, 4 - o), rel(z, j), x_peer[o])

    def cot_pair(o):
        part = cot.at[rel(x, o), :, c]
        push("cot_c", 0, part, part, core_peer)

    order = (2, 1, 3, 0)

    def columns(k, oz, ox, cc):
        start = ((rel(z, oz) * 4 + rel(x, ox)) * 2 + cc) * 256 + k * 128
        return q[:, pl.ds(pl.multiple_of(start, 128), 128)]

    def block(k, ox, j, cc):
        return dot(act[...], columns(k, order[j], ox, cc), ((1,), (0,)))

    def send_core(k):
        for ox in (2, 3, 1, 0):
            for j in range(4):
                send_c[k, ox, j] = block(k, ox, j, other).astype(BF16)
            push("core", (k, ox), send_c.at[k, ox], recv_c.at[k, ox], core_peer)

    def pair_sum(k, ox, j):
        return block(k, ox, j, c) + recv_c[k, ox, j].astype(F32)

    def send_far(k, j):
        out2[k, j] = pair_sum(k, 2, j).astype(BF16)
        push("far", (k, j), out2.at[k, j], recv2.at[k, j], x_peer[1 if j < 2 else 3])

    def send_plus(k, j):
        total_j = pair_sum(k, 1, j)
        if j < 2:
            need("far", (k, j), recv2.at[k, j])
            total_j = total_j + recv2[k, j].astype(F32)
        out1p[k, j] = total_j.astype(BF16)
        push("near_x", (k, j), out1p.at[k, j], recv1m.at[k, j], x_peer[1])

    def send_minus(k, j):
        total_j = pair_sum(k, 3, j)
        if j >= 2:
            need("far", (k, j), recv2.at[k, j])
            total_j = total_j + recv2[k, j].astype(F32)
        out1m[k, j] = total_j.astype(BF16)
        push("near_x", (k, j), out1m.at[k, j], recv1p.at[k, j], x_peer[3])

    def send_first(k):
        need("core", (k, 2), recv_c.at[k, 2])
        for j in (0, 2, 1, 3):
            send_far(k, j)
        need("core", (k, 3), recv_c.at[k, 3])
        send_minus(k, 0)
        send_minus(k, 1)
        need("core", (k, 1), recv_c.at[k, 1])
        send_plus(k, 2)
        send_plus(k, 3)

    def send_second(k):
        send_plus(k, 0)
        send_minus(k, 2)
        send_plus(k, 1)
        send_minus(k, 3)

    def send_z(k):
        need("core", (k, 0), recv_c.at[k, 0])
        for j in range(4):
            total_j = pair_sum(k, 0, j)
            need("near_x", (k, j), recv1m.at[k, 0:2])
            total_j = total_j + recv1m[k, j].astype(F32) + recv1p[k, j].astype(F32)
            if order[j]:
                out_z[k, j] = total_j.astype(BF16)
                push("near_z", k, out_z.at[k, j], recv_z.at[k, j], z_peer[order[j]])
            else:
                total[k] = total_j

    def rot_to_y(k, j):
        block_j = rot.at[k, rel(h, j), y]
        for o in (2, 1, 3):
            push("rot_y", (k, j), block_j, block_j, y_peer[o])

    def rot_own(k):
        need("near_z", k, recv_z.at[k])
        sum_k = total[k]
        for j in range(3):
            sum_k = sum_k + recv_z[k, j].astype(F32)
        rot[k, h, y] = sum_k.astype(BF16)
        for o in (1, 3):
            push("rot_h", (k, o), rot.at[k, h, y], rot.at[k, h, y], h_peer[o])
        rot_to_y(k, 0)

    def rot_next(k):
        for o in (1, 3):
            need("rot_h", (k, o), rot.at[k, 0, 0])
            lo = 0 if o == 1 else 112
            part = rot.at[k, rel(h, 4 - o), y, lo : lo + 112]
            push("rot_h", (k, 2), part, part, h_peer[o])
            rot_to_y(k, 4 - o)

    def rot_last(k):
        need("rot_h", (k, 2), rot.at[k, 0, 0])
        rot_to_y(k, 2)

    def add_tokens(k, j):
        need("rot_y", (k, j), rot.at[k, 0, 0:3])
        hh = rel(h, j)
        part = dot(rot[k, hh].reshape(896, 128), cot[hh].reshape(896, 256), ((0,), (0,)))
        if j == 0:
            moment[k] = part
        else:
            moment[k] += part

    def gather_own(k):
        s[k, 0, 0, c] = (moment[k] * scale[k * 128 : (k + 1) * 128, :]).astype(BF16)
        mine = s.at[k, 0, 0, c]
        for o in (2, 1, 3):
            push("s_z", (k, o), mine, s.at[k, 0, 4 - o, c], z_peer[o])
        for o in (1, 3):
            push("s_x", (k, 0), mine, s.at[k, 4 - o, 0, c], x_peer[o])

    def gather_z(k, o):
        need("s_z", (k, o), s.at[k, 0, 0, 0])
        j = 4 - o
        for ox in (1, 3):
            push("s_x", (k, j), s.at[k, 0, j, c], s.at[k, 4 - ox, j, c], x_peer[ox])

    def gather_pair(k, ox, lo, hi):
        part = s.at[k, ox, lo:hi, c]
        push("s_c", (k, ox, lo), part, part, core_peer)

    def gather_forward(k, j):
        need("s_x", (k, j), s.at[k, 0, 0:2, 0])
        o = 1 if j < 2 else 3
        push("s_f", (k, j // 2), s.at[k, 4 - o, j, c], s.at[k, 2, j, c], x_peer[o])

    def add_blocks(k, ox, lo, hi):
        need("s_c", (k, ox, lo), s.at[k, 0, 0 : hi - lo, 0])
        sum_j = jnp.zeros((256, 256), F32)
        for j in range(lo, hi):
            for cc in (0, 1):
                sum_j = sum_j + dot(columns(k, j, ox, cc), s[k, ox, j, cc], ((1,), (0,)))
        if k == 0 and ox == 0:
            acc[...] = sum_j
        else:
            acc[...] += sum_j

    lane = lax.broadcasted_iota(jnp.int32, (16, 2 * PANEL), 1)
    row = lax.broadcasted_iota(jnp.int32, (16, PANEL), 0)

    def eliminate(b):
        k0 = 16 * b
        left = chol[k0 : k0 + 16, :PANEL]
        right = chol[k0 : k0 + 16, PANEL:]
        wide = [jnp.broadcast_to(left[:, k0 + j : k0 + j + 1], (16, PANEL)) for j in range(16)]
        for i in range(16):
            pivot = wide[i][i : i + 1, :]
            inv = lax.rsqrt(pivot)
            inv = inv * (1.5 - 0.5 * pivot * inv * inv)
            below = jnp.where(row > i, wide[i] * inv, 0.0)
            for j in range(i + 1, 16):
                wide[j] = wide[j] - below * (wide[j][i : i + 1, :] * inv)
            left_row = left[i : i + 1, :] * inv
            right_row = right[i : i + 1, :] * inv
            left = jnp.where(row == i, left_row, left - below * left_row)
            right = jnp.where(row == i, right_row, right - below * right_row)
        r = jnp.concatenate([left, right], axis=1)
        chol[k0 : k0 + 16, :] = r
        if b < 7:
            r = jnp.where(lane >= k0 + 16, r, 0.0)
            hi = r.astype(BF16)
            rest = r - hi.astype(F32)
            mid = rest.astype(BF16)
            low = (rest - mid.astype(F32)).astype(BF16)
            first = jnp.concatenate([hi, hi, hi, mid, mid, low], axis=0)[:, :PANEL]
            second = jnp.concatenate([hi, mid, low, hi, mid, hi], axis=0)
            chol[k0 + 16 :, :] -= dot(first, second, ((0,), (0,)))[k0 + 16 :, :]

    def panel_y():
        need("pan_h", 0, pan.at[0, 0:3])
        for o in (1, 2, 3):
            push("pan_y", 0, pan.at[:, y], pan.at[:, y], y_peer[o])

    def image_core():
        need("pan_y", 0, pan.at[0:3])
        loads[4].wait()
        pan_t = pan[...].transpose(1, 0, 2, 3).reshape(PANEL, 256)
        im_part[...] = dot(f[...], pan_t, ((1,), (1,)), HIGHEST).reshape(4, 4, 2, 16, PANEL)
        push("im_core", 0, im_part.at[:, :, other], im_c, core_peer)

    def image_x():
        need("im_core", 0, im_c)
        im_s[...] = im_part[:, :, c] + im_c[...]
        for o in (1, 2, 3):
            push("im_xc", 0, im_s.at[:, rel(x, o)], im_x.at[o], x_peer[o])

    def image_z():
        need("im_xc", 0, im_x.at[1:4])
        im_xs[...] = im_s[:, x] + im_x[1] + im_x[2] + im_x[3]
        for o in (1, 2, 3):
            push("im_zc", 0, im_xs.at[rel(z, o)], im_z.at[o], z_peer[o])

    def gram_core():
        need("im_zc", 0, im_z.at[1:4])
        image = im_xs[z] + im_z[1] + im_z[2] + im_z[3]
        gr[...] = dot(image, image, ((0,), (0,)), HIGHEST) * (1.0 / D)
        chol[:, PANEL:] = jnp.concatenate([image, jnp.zeros((PANEL - 16, PANEL), F32)], axis=0).T
        push("gr_core", 0, gr.at[pl.ds(pl.multiple_of(other * 64, 64), 64)], gr_c, core_peer)

    def gram_x():
        need("gr_core", 0, gr_c)
        gr_h[...] = gr[pl.ds(pl.multiple_of(c * 64, 64), 64), :] + gr_c[...]
        for o in (1, 2, 3):
            share = pl.ds(pl.multiple_of(rel(x, o) * 16, 16), 16)
            push("gr_xc", 0, gr_h.at[share], gr_x.at[o], x_peer[o])

    def gram_z():
        need("gr_xc", 0, gr_x.at[1:4])
        mine = gr_h[pl.ds(pl.multiple_of(x * 16, 16), 16), :]
        gr_q[...] = mine + gr_x[1] + gr_x[2] + gr_x[3]
        for o in (1, 2, 3):
            push("gr_zc", 0, gr_q, gr_l.at[o], z_peer[o])

    def gram_y():
        need("gr_zc", 0, gr_l.at[1:4])
        gr_l2[...] = gr_q[...] + gr_l[1] + gr_l[2] + gr_l[3]
        for o in (1, 2, 3):
            push("gr_yc", 0, gr_l2, gr_y.at[o], y_peer[o])

    def gram_h():
        need("gr_yc", 0, gr_y.at[1:4])
        gr_y2[...] = gr_l2[...] + gr_y[1] + gr_y[2] + gr_y[3]
        for o in (1, 2, 3):
            push("gr_hc", 0, gr_y2, gr_z.at[o], h_peer[o])

    def gram_x_back():
        need("gr_hc", 0, gr_z.at[1:4])
        lo = pl.ds(pl.multiple_of(c * 64 + x * 16, 16), 16)
        gr_full[lo, :] = gr_y2[...] + gr_z[1] + gr_z[2] + gr_z[3]
        for o in (1, 2, 3):
            push("gr_xg", 0, gr_full.at[lo], gr_full.at[lo], x_peer[o])

    def gram_core_back():
        need("gr_xg", 0, gr_full.at[0:48])
        half = pl.ds(pl.multiple_of(c * 64, 64), 64)
        push("gr_cg", 0, gr_full.at[half], gr_full.at[half], core_peer)

    for o in (2, 1, 3):
        push("pan_h", 0, pan.at[h, y], pan.at[h, y], h_peer[o])
    for o in (2, 1, 3):
        cot_push("cot_z", o, x, z, z_peer[o])
    loads[2].wait()
    loads[3].wait()
    send_core(0)
    send_first(0)
    send_core(1)
    loads[5].wait()
    scale[...] = (1.0 / TOKENS) / (v[...].astype(F32) + DAMPING)
    panel_y()
    send_second(0)
    send_first(1)
    send_z(0)
    image_core()
    send_second(1)
    image_x()
    for o in (1, 3):
        cot_push("cot_x", 0, x, z, x_peer[o])
    for o in (1, 3, 2):
        need("cot_z", o, cot.at[0, 0, 0])
        for ox in (1, 3):
            cot_push("cot_x", 4 - o, x, rel(z, 4 - o), x_peer[ox])
    cot_pair(0)
    rot_own(0)
    image_z()
    send_z(1)
    for j in (0, 3, 1, 2):
        cot_forward(j)
    cot_pair(1)
    cot_pair(3)
    gram_core()
    rot_next(0)
    gram_x()
    rot_own(1)
    need("cot_f", 0, cot.at[:, 0, 0])
    cot_pair(2)
    gram_z()
    rot_last(0)
    gram_y()
    need("cot_c", 0, cot.at[:, :, 0])
    rot_next(1)
    for j in (0, 3, 1, 2):
        add_tokens(0, j)
    gather_own(0)
    gram_h()
    rot_last(1)
    gather_z(0, 1)
    gather_z(0, 3)
    gather_z(0, 2)
    gather_pair(0, 0, 0, 4)
    for j in (0, 3, 1, 2):
        add_tokens(1, j)
    gather_own(1)
    gram_x_back()
    gather_forward(0, 0)
    gather_forward(0, 3)
    gather_forward(0, 1)
    gather_forward(0, 2)
    gather_pair(0, 1, 0, 4)
    gather_pair(0, 3, 0, 4)
    gram_core_back()
    gather_z(1, 1)
    gather_z(1, 3)
    need("gr_cg", 0, gr_full.at[0:64])
    chol[:, :PANEL] = gr_full[...]
    gather_z(1, 2)
    gather_pair(1, 0, 0, 4)
    eliminate(0)
    eliminate(1)
    need("s_f", (0, 0), s.at[0, 0, 0:2, 0])
    gather_pair(0, 2, 0, 2)
    need("s_f", (0, 1), s.at[0, 0, 0:2, 0])
    gather_pair(0, 2, 2, 4)
    eliminate(2)
    eliminate(3)
    gather_forward(1, 0)
    gather_forward(1, 3)
    eliminate(4)
    eliminate(5)
    add_blocks(0, 0, 0, 4)
    gather_forward(1, 1)
    gather_forward(1, 2)
    gather_pair(1, 1, 0, 4)
    gather_pair(1, 3, 0, 4)
    add_blocks(0, 1, 0, 4)
    add_blocks(0, 3, 0, 4)
    add_blocks(0, 2, 0, 2)
    add_blocks(0, 2, 2, 4)
    add_blocks(1, 0, 0, 4)
    eliminate(6)
    need("s_f", (1, 0), s.at[1, 0, 0:2, 0])
    gather_pair(1, 2, 0, 2)
    need("s_f", (1, 1), s.at[1, 0, 0:2, 0])
    gather_pair(1, 2, 2, 4)
    eliminate(7)
    new_ref[...] = chol[:, PANEL:].T[:16, :]
    add_blocks(1, 1, 0, 4)
    add_blocks(1, 3, 0, 4)
    add_blocks(1, 2, 0, 2)
    add_blocks(1, 2, 2, 4)
    upd_ref[...] = acc[...].astype(BF16)
    bytes_like = {
        "pan_h": pan.at[0, 0:3], "pan_y": pan.at[0:3], "im_core": im_c, "im_xc": im_x.at[1:4],
        "im_zc": im_z.at[1:4], "gr_core": gr_c, "gr_xc": gr_x.at[1:4], "gr_zc": gr_l.at[1:4],
        "gr_yc": gr_y.at[1:4], "gr_hc": gr_z.at[1:4], "gr_xg": gr_full.at[0:48],
        "gr_cg": gr_full.at[0:64], "cot_z": cot.at[0, 0:3, 0], "cot_x": cot.at[:, 0:2, 0],
        "cot_f": cot.at[:, 0, 0], "cot_c": cot.at[:, :, 0], "core": send_c, "far": out2,
        "near_x": send_c.at[:, 0:2], "near_z": out_z, "rot_h": rot.at[:, 0, 0:3],
        "rot_y": rot.at[:, 0:3], "s_z": s.at[:, 0, 0:3, 0], "s_x": s.at[:, 0:2, :, 0],
        "s_f": s.at[:, 0, :, 0], "s_c": s.at[:, :, :, 0],
    }
    for group, entry in sent.items():
        wait_bytes(send_sem, entry, bytes_like[group])
    assert len(sent) <= N_SENT and len(received) <= N_RECEIVED
    assert not any(size for _, size in received.values())


def body(activations, cotangent, eigenbasis, second_moment, factor, old_panel):
    vmem = pl.BlockSpec(memory_space=pltpu.VMEM)
    hbm = pl.BlockSpec(memory_space=pl.ANY)
    tile = (224, 128)
    half = (128, 256)
    part = (16, PANEL)
    scratch = [
        pltpu.VMEM((256, D), BF16),
        pltpu.VMEM((512, 256), F32),
        pltpu.VMEM((256, 256), BF16),
        pltpu.VMEM((224, 256), BF16),
        pltpu.VMEM((2, 4, 4) + tile, BF16),
        pltpu.VMEM((4, 4, 2, 112, 256), BF16),
        pltpu.VMEM((4, 4, 8, 256), F32),
        pltpu.VMEM((256, 256), F32),
        pltpu.VMEM((2,) + half, F32),
        pltpu.VMEM((2, 4, 4) + tile, BF16),
        pltpu.VMEM((2, 4, 4) + tile, BF16),
        pltpu.VMEM((2, 4) + tile, BF16),
        pltpu.VMEM((2, 4) + tile, BF16),
        pltpu.VMEM((2, 4) + tile, BF16),
        pltpu.VMEM((2, 4) + tile, BF16),
        pltpu.VMEM((2, 4) + tile, BF16),
        pltpu.VMEM((2, 4) + tile, BF16),
        pltpu.VMEM((2, 3) + tile, BF16),
        pltpu.VMEM((2, 3) + tile, BF16),
        pltpu.VMEM((2,) + tile, F32),
        pltpu.VMEM((2, 4, 4, 2) + half, BF16),
        pltpu.VMEM((256, 256), F32),
        pltpu.VMEM((4, 4, 2) + part, F32),
        pltpu.VMEM((4, 4) + part, F32),
        pltpu.VMEM((4, 4) + part, F32),
        pltpu.VMEM((4, 4) + part, F32),
        pltpu.VMEM((4,) + part, F32),
        pltpu.VMEM((4,) + part, F32),
        pltpu.VMEM((PANEL, PANEL), F32),
        pltpu.VMEM((64, PANEL), F32),
        pltpu.VMEM((64, PANEL), F32),
        pltpu.VMEM((4,) + part, F32),
        pltpu.VMEM(part, F32),
        pltpu.VMEM((4,) + part, F32),
        pltpu.VMEM(part, F32),
        pltpu.VMEM((4,) + part, F32),
        pltpu.VMEM(part, F32),
        pltpu.VMEM((4,) + part, F32),
        pltpu.VMEM((PANEL, PANEL), F32),
        pltpu.VMEM((PANEL, 2 * PANEL), F32),
        pltpu.SemaphoreType.DMA((N_SENT,)),
        pltpu.SemaphoreType.DMA((N_RECEIVED,)),
        pltpu.SemaphoreType.DMA((6,)),
    ]
    return pl.pallas_call(
        kernel,
        out_shape=(
            jax.ShapeDtypeStruct((256, 256), BF16),
            jax.ShapeDtypeStruct(part, F32),
        ),
        in_specs=[hbm] * 6,
        out_specs=(vmem, vmem),
        scratch_shapes=scratch,
        compiler_params=pltpu.CompilerParams(
            collective_id=0, has_side_effects=True, vmem_limit_bytes=60 * 1024 * 1024
        ),
    )(
        activations, cotangent, eigenbasis, second_moment, factor, old_panel.T
    )


def solution(mesh):
    return jax.shard_map(
        body,
        mesh=mesh,
        in_specs=(
            P("grp", "dev"),
            P("dev", "grp"),
            P("dev", None),
            P("dev", "grp"),
            P("grp", "dev"),
            P("dev", "grp"),
        ),
        out_specs=(P("dev", "grp"), P(("grp", "dev"), None)),
        check_vma=False,
    )
```

```python
import math

import jax
import jax.numpy as jnp
from jax import lax
from jax.experimental import pallas as pl
from jax.experimental.pallas import tpu as pltpu
from jax.sharding import PartitionSpec as P

D = 8192
TOKENS = 3584
PANEL = 128
DAMPING = 0.01
MESH = pl.DeviceIdType.MESH
F32, BF16 = jnp.float32, jnp.bfloat16
HIGHEST = lax.Precision.HIGHEST

N_SENT = 26
N_RECEIVED = 89


def dot(a, b, dims, precision=None):
    return lax.dot_general(a, b, (dims, ((), ())), precision=precision, preferred_element_type=F32)


def rel(i, o):
    return lax.rem(i + o, 4)


def kernel(
    a_hbm, c_hbm, q_hbm, v_hbm, f_hbm, p_hbm, upd_ref, new_ref,
    q, f, v, act, rot, cot, pan, scale, moment,
    send_c, recv_c, out2, recv2, out1p, out1m, recv1m, recv1p, out_z, recv_z, total, s, acc,
    im_part, im_c, im_s, im_x, im_xs, im_z,
    gr, gr_c, gr_h, gr_x, gr_q, gr_l, gr_l2, gr_y, gr_y2, gr_z, gr_full, chol,
    send_sem, recv_sem, local_sem,
):
    grp, dev = lax.axis_index("grp"), lax.axis_index("dev")
    y, h = grp // 4, lax.rem(grp, 4)
    c = lax.rem(dev, 2)
    x = lax.rem(dev // 2, 4)
    z = dev // 8
    other = 1 - c

    def at(yy=y, hh=h, zz=z, xx=x, cc=c):
        return (yy * 4 + hh, (zz * 4 + xx) * 2 + cc)

    core_peer = at(cc=other)
    x_peer = {o: at(xx=rel(x, o)) for o in (1, 2, 3)}
    z_peer = {o: at(zz=rel(z, o)) for o in (1, 2, 3)}
    y_peer = {o: at(yy=rel(y, o)) for o in (1, 2, 3)}
    h_peer = {o: at(hh=rel(h, o)) for o in (1, 2, 3)}
    peers = [core_peer]
    for table in (x_peer, z_peer, y_peer, h_peer):
        peers += [table[o] for o in (1, 2, 3)]

    barrier = pltpu.get_barrier_semaphore()
    for peer in peers:
        pl.semaphore_signal(barrier, inc=1, device_id=peer, device_id_type=MESH)

    pairs = (
        (p_hbm, pan.at[h, y]), (c_hbm, cot.at[x, z, c]), (a_hbm, act),
        *((q_hbm.at[n : n + 64], q.at[n : n + 64]) for n in range(0, 256, 64)),
        (f_hbm, f), (v_hbm, v),
    )
    loads = [pltpu.make_async_copy(src, dst, local_sem.at[n]) for n, (src, dst) in enumerate(pairs)]
    for load in loads:
        load.start()
    for load in loads[:2]:
        load.wait()
    pl.semaphore_wait(barrier, len(peers))

    sent, received = {}, {}

    def push(group, key, src, dst, peer):
        copy = pltpu.make_async_remote_copy(
            src_ref=src, dst_ref=dst,
            send_sem=send_sem.at[sent.setdefault(group, [len(sent), 0])[0]],
            recv_sem=recv_sem.at[received.setdefault((group, key), [len(received), 0])[0]],
            device_id=peer, device_id_type=MESH,
        )
        copy.start()
        size = math.prod(src.shape) * src.dtype.itemsize
        sent[group][1] += size
        received[group, key][1] += size

    def wait_bytes(semaphore, entry, like):
        assert entry[1] == math.prod(like.shape) * like.dtype.itemsize
        entry[1] = 0
        pltpu.make_async_copy(like, like, semaphore.at[entry[0]]).wait()

    def need(group, key, like):
        wait_bytes(recv_sem, received[group, key], like)

    def cot_push(group, key, xx, zz, peer):
        push(group, key, cot.at[xx, zz, c], cot.at[xx, zz, c], peer)

    def cot_forward(j):
        need("cot_x", j, cot.at[0, 0:2, 0])
        o = 1 if j < 2 else 3
        cot_push("cot_f", 0, rel(x, 4 - o), rel(z, j), x_peer[o])

    def cot_pair(o):
        part = cot.at[rel(x, o), :, c]
        push("cot_c", 0, part, part, core_peer)

    order = (2, 1, 3, 0)

    def columns(k, oz, ox, cc):
        start = ((rel(z, oz) * 4 + rel(x, ox)) * 2 + cc) * 256 + k * 128
        return q[:, pl.ds(pl.multiple_of(start, 128), 128)]

    def block(k, ox, j, cc):
        return dot(act[...], columns(k, order[j], ox, cc), ((1,), (0,)))

    def send_core(k):
        for ox in (2, 3, 1, 0):
            for j in range(4):
                send_c[k, ox, j] = block(k, ox, j, other).astype(BF16)
            push("core", (k, ox), send_c.at[k, ox], recv_c.at[k, ox], core_peer)

    def pair_sum(k, ox, j):
        return block(k, ox, j, c) + recv_c[k, ox, j].astype(F32)

    def send_far(k, j):
        out2[k, j] = pair_sum(k, 2, j).astype(BF16)
        push("far", (k, j), out2.at[k, j], recv2.at[k, j], x_peer[1 if j < 2 else 3])

    def send_plus(k, j):
        total_j = pair_sum(k, 1, j)
        if j < 2:
            need("far", (k, j), recv2.at[k, j])
            total_j = total_j + recv2[k, j].astype(F32)
        out1p[k, j] = total_j.astype(BF16)
        push("near_x", (k, j), out1p.at[k, j], recv1m.at[k, j], x_peer[1])

    def send_minus(k, j):
        total_j = pair_sum(k, 3, j)
        if j >= 2:
            need("far", (k, j), recv2.at[k, j])
            total_j = total_j + recv2[k, j].astype(F32)
        out1m[k, j] = total_j.astype(BF16)
        push("near_x", (k, j), out1m.at[k, j], recv1p.at[k, j], x_peer[3])

    def send_first(k):
        need("core", (k, 2), recv_c.at[k, 2])
        for j in (0, 2, 1, 3):
            send_far(k, j)
        need("core", (k, 3), recv_c.at[k, 3])
        send_minus(k, 0)
        send_minus(k, 1)
        need("core", (k, 1), recv_c.at[k, 1])
        send_plus(k, 2)
        send_plus(k, 3)

    def send_second(k):
        send_plus(k, 0)
        send_minus(k, 2)
        send_plus(k, 1)
        send_minus(k, 3)

    def send_z(k):
        need("core", (k, 0), recv_c.at[k, 0])
        for j in range(4):
            total_j = pair_sum(k, 0, j)
            need("near_x", (k, j), recv1m.at[k, 0:2])
            total_j = total_j + recv1m[k, j].astype(F32) + recv1p[k, j].astype(F32)
            if order[j]:
                out_z[k, j] = total_j.astype(BF16)
                push("near_z", k, out_z.at[k, j], recv_z.at[k, j], z_peer[order[j]])
            else:
                total[k] = total_j

    def rot_to_y(k, j):
        block_j = rot.at[k, rel(h, j), y]
        for o in (2, 1, 3):
            push("rot_y", (k, j), block_j, block_j, y_peer[o])

    def rot_own(k):
        need("near_z", k, recv_z.at[k])
        sum_k = total[k]
        for j in range(3):
            sum_k = sum_k + recv_z[k, j].astype(F32)
        rot[k, h, y] = sum_k.astype(BF16)
        for o in (1, 3):
            push("rot_h", (k, o), rot.at[k, h, y], rot.at[k, h, y], h_peer[o])
        rot_to_y(k, 0)

    def rot_next(k):
        for o in (1, 3):
            need("rot_h", (k, o), rot.at[k, 0, 0])
            lo = 0 if o == 1 else 112
            part = rot.at[k, rel(h, 4 - o), y, lo : lo + 112]
            push("rot_h", (k, 2), part, part, h_peer[o])
            rot_to_y(k, 4 - o)

    def rot_last(k):
        need("rot_h", (k, 2), rot.at[k, 0, 0])
        rot_to_y(k, 2)

    def add_tokens(k, j):
        need("rot_y", (k, j), rot.at[k, 0, 0:3])
        hh = rel(h, j)
        part = dot(rot[k, hh].reshape(896, 128), cot[hh].reshape(896, 256), ((0,), (0,)))
        if j == 0:
            moment[k] = part
        else:
            moment[k] += part

    def gather_own(k):
        s[k, 0, 0, c] = (moment[k] * scale[k * 128 : (k + 1) * 128, :]).astype(BF16)
        mine = s.at[k, 0, 0, c]
        for o in (2, 1, 3):
            push("s_z", (k, o), mine, s.at[k, 0, 4 - o, c], z_peer[o])
        for o in (1, 3):
            push("s_x", (k, 0), mine, s.at[k, 4 - o, 0, c], x_peer[o])

    def gather_z(k, o):
        need("s_z", (k, o), s.at[k, 0, 0, 0])
        j = 4 - o
        for ox in (1, 3):
            push("s_x", (k, j), s.at[k, 0, j, c], s.at[k, 4 - ox, j, c], x_peer[ox])

    def gather_pair(k, ox, lo, hi):
        part = s.at[k, ox, lo:hi, c]
        push("s_c", (k, ox, lo), part, part, core_peer)

    def gather_forward(k, j):
        need("s_x", (k, j), s.at[k, 0, 0:2, 0])
        o = 1 if j < 2 else 3
        push("s_f", (k, j // 2), s.at[k, 4 - o, j, c], s.at[k, 2, j, c], x_peer[o])

    def add_blocks(k, ox, lo, hi):
        need("s_c", (k, ox, lo), s.at[k, 0, 0 : hi - lo, 0])
        sum_j = jnp.zeros((256, 256), F32)
        for j in range(lo, hi):
            for cc in (0, 1):
                sum_j = sum_j + dot(columns(k, j, ox, cc), s[k, ox, j, cc], ((1,), (0,)))
        if k == 0 and ox == 0:
            acc[...] = sum_j
        else:
            acc[...] += sum_j

    lane = lax.broadcasted_iota(jnp.int32, (16, 2 * PANEL), 1)
    row = lax.broadcasted_iota(jnp.int32, (16, PANEL), 0)

    def eliminate(b):
        k0 = 16 * b
        left = chol[k0 : k0 + 16, :PANEL]
        right = chol[k0 : k0 + 16, PANEL:]
        wide = [jnp.broadcast_to(left[:, k0 + j : k0 + j + 1], (16, PANEL)) for j in range(16)]
        for i in range(16):
            pivot = wide[i][i : i + 1, :]
            inv = lax.rsqrt(pivot)
            inv = inv * (1.5 - 0.5 * pivot * inv * inv)
            below = jnp.where(row > i, wide[i] * inv, 0.0)
            for j in range(i + 1, 16):
                wide[j] = wide[j] - below * (wide[j][i : i + 1, :] * inv)
            left_row = left[i : i + 1, :] * inv
            right_row = right[i : i + 1, :] * inv
            left = jnp.where(row == i, left_row, left - below * left_row)
            right = jnp.where(row == i, right_row, right - below * right_row)
        r = jnp.concatenate([left, right], axis=1)
        chol[k0 : k0 + 16, :] = r
        if b < 7:
            r = jnp.where(lane >= k0 + 16, r, 0.0)
            hi = r.astype(BF16)
            rest = r - hi.astype(F32)
            mid = rest.astype(BF16)
            low = (rest - mid.astype(F32)).astype(BF16)
            first = jnp.concatenate([hi, hi, hi, mid, mid, low], axis=0)[:, :PANEL]
            second = jnp.concatenate([hi, mid, low, hi, mid, hi], axis=0)
            chol[k0 + 16 :, :] -= dot(first, second, ((0,), (0,)))[k0 + 16 :, :]

    def panel_y():
        need("pan_h", 0, pan.at[0, 0:3])
        for o in (1, 2, 3):
            push("pan_y", 0, pan.at[:, y], pan.at[:, y], y_peer[o])

    def image_core():
        need("pan_y", 0, pan.at[0:3])
        loads[7].wait()
        pan_t = pan[...].transpose(1, 0, 2, 3).reshape(PANEL, 256)
        im_part[...] = dot(f[...], pan_t, ((1,), (1,)), HIGHEST).reshape(4, 4, 2, 16, PANEL)
        push("im_core", 0, im_part.at[:, :, other], im_c, core_peer)

    def image_x():
        need("im_core", 0, im_c)
        im_s[...] = im_part[:, :, c] + im_c[...]
        for o in (1, 2, 3):
            push("im_xc", 0, im_s.at[:, rel(x, o)], im_x.at[o], x_peer[o])

    def image_z():
        need("im_xc", 0, im_x.at[1:4])
        im_xs[...] = im_s[:, x] + im_x[1] + im_x[2] + im_x[3]
        for o in (1, 2, 3):
            push("im_zc", 0, im_xs.at[rel(z, o)], im_z.at[o], z_peer[o])

    def gram_core():
        need("im_zc", 0, im_z.at[1:4])
        image = im_xs[z] + im_z[1] + im_z[2] + im_z[3]
        gr[...] = dot(image, image, ((0,), (0,)), HIGHEST) * (1.0 / D)
        chol[:, PANEL:] = jnp.concatenate([image, jnp.zeros((PANEL - 16, PANEL), F32)], axis=0).T
        push("gr_core", 0, gr.at[pl.ds(pl.multiple_of(other * 64, 64), 64)], gr_c, core_peer)

    def gram_x():
        need("gr_core", 0, gr_c)
        gr_h[...] = gr[pl.ds(pl.multiple_of(c * 64, 64), 64), :] + gr_c[...]
        for o in (1, 2, 3):
            share = pl.ds(pl.multiple_of(rel(x, o) * 16, 16), 16)
            push("gr_xc", 0, gr_h.at[share], gr_x.at[o], x_peer[o])

    def gram_z():
        need("gr_xc", 0, gr_x.at[1:4])
        mine = gr_h[pl.ds(pl.multiple_of(x * 16, 16), 16), :]
        gr_q[...] = mine + gr_x[1] + gr_x[2] + gr_x[3]
        for o in (1, 2, 3):
            push("gr_zc", 0, gr_q, gr_l.at[o], z_peer[o])

    def gram_y():
        need("gr_zc", 0, gr_l.at[1:4])
        gr_l2[...] = gr_q[...] + gr_l[1] + gr_l[2] + gr_l[3]
        for o in (1, 2, 3):
            push("gr_yc", 0, gr_l2, gr_y.at[o], y_peer[o])

    def gram_h():
        need("gr_yc", 0, gr_y.at[1:4])
        gr_y2[...] = gr_l2[...] + gr_y[1] + gr_y[2] + gr_y[3]
        for o in (1, 2, 3):
            push("gr_hc", 0, gr_y2, gr_z.at[o], h_peer[o])

    def gram_x_back():
        need("gr_hc", 0, gr_z.at[1:4])
        lo = pl.ds(pl.multiple_of(c * 64 + x * 16, 16), 16)
        gr_full[lo, :] = gr_y2[...] + gr_z[1] + gr_z[2] + gr_z[3]
        for o in (1, 2, 3):
            push("gr_xg", 0, gr_full.at[lo], gr_full.at[lo], x_peer[o])

    def gram_core_back():
        need("gr_xg", 0, gr_full.at[0:48])
        half = pl.ds(pl.multiple_of(c * 64, 64), 64)
        push("gr_cg", 0, gr_full.at[half], gr_full.at[half], core_peer)

    for o in (2, 1, 3):
        push("pan_h", 0, pan.at[h, y], pan.at[h, y], h_peer[o])
    for o in (2, 1, 3):
        cot_push("cot_z", o, x, z, z_peer[o])
    for load in loads[2:7]:
        load.wait()
    send_core(0)
    send_first(0)
    send_core(1)
    loads[8].wait()
    scale[...] = (1.0 / TOKENS) / (v[...].astype(F32) + DAMPING)
    panel_y()
    send_second(0)
    send_first(1)
    send_z(0)
    image_core()
    send_second(1)
    image_x()
    for o in (1, 3):
        cot_push("cot_x", 0, x, z, x_peer[o])
    for o in (1, 3, 2):
        need("cot_z", o, cot.at[0, 0, 0])
        for ox in (1, 3):
            cot_push("cot_x", 4 - o, x, rel(z, 4 - o), x_peer[ox])
    cot_pair(0)
    rot_own(0)
    image_z()
    send_z(1)
    for j in (0, 3, 1, 2):
        cot_forward(j)
    cot_pair(1)
    cot_pair(3)
    gram_core()
    rot_next(0)
    gram_x()
    rot_own(1)
    need("cot_f", 0, cot.at[:, 0, 0])
    cot_pair(2)
    gram_z()
    rot_last(0)
    gram_y()
    need("cot_c", 0, cot.at[:, :, 0])
    rot_next(1)
    for j in (0, 3, 1, 2):
        add_tokens(0, j)
    gather_own(0)
    gram_h()
    rot_last(1)
    gather_z(0, 1)
    gather_z(0, 3)
    gather_z(0, 2)
    gather_pair(0, 0, 0, 4)
    for j in (0, 3, 1, 2):
        add_tokens(1, j)
    gather_own(1)
    gram_x_back()
    gather_forward(0, 0)
    gather_forward(0, 3)
    gather_forward(0, 1)
    gather_forward(0, 2)
    gather_pair(0, 1, 0, 4)
    gather_pair(0, 3, 0, 4)
    gram_core_back()
    gather_z(1, 1)
    gather_z(1, 3)
    need("gr_cg", 0, gr_full.at[0:64])
    chol[:, :PANEL] = gr_full[...]
    gather_z(1, 2)
    gather_pair(1, 0, 0, 4)
    eliminate(0)
    eliminate(1)
    need("s_f", (0, 0), s.at[0, 0, 0:2, 0])
    gather_pair(0, 2, 0, 2)
    need("s_f", (0, 1), s.at[0, 0, 0:2, 0])
    gather_pair(0, 2, 2, 4)
    eliminate(2)
    eliminate(3)
    gather_forward(1, 0)
    gather_forward(1, 3)
    eliminate(4)
    eliminate(5)
    add_blocks(0, 0, 0, 4)
    gather_forward(1, 1)
    gather_forward(1, 2)
    gather_pair(1, 1, 0, 4)
    gather_pair(1, 3, 0, 4)
    add_blocks(0, 1, 0, 4)
    add_blocks(0, 3, 0, 4)
    add_blocks(0, 2, 0, 2)
    add_blocks(0, 2, 2, 4)
    add_blocks(1, 0, 0, 4)
    eliminate(6)
    need("s_f", (1, 0), s.at[1, 0, 0:2, 0])
    gather_pair(1, 2, 0, 2)
    need("s_f", (1, 1), s.at[1, 0, 0:2, 0])
    gather_pair(1, 2, 2, 4)
    eliminate(7)
    new_ref[...] = chol[:, PANEL:].T[:16, :]
    add_blocks(1, 1, 0, 4)
    add_blocks(1, 3, 0, 4)
    add_blocks(1, 2, 0, 2)
    add_blocks(1, 2, 2, 4)
    upd_ref[...] = acc[...].astype(BF16)
    bytes_like = {
        "pan_h": pan.at[0, 0:3], "pan_y": pan.at[0:3], "im_core": im_c, "im_xc": im_x.at[1:4],
        "im_zc": im_z.at[1:4], "gr_core": gr_c, "gr_xc": gr_x.at[1:4], "gr_zc": gr_l.at[1:4],
        "gr_yc": gr_y.at[1:4], "gr_hc": gr_z.at[1:4], "gr_xg": gr_full.at[0:48],
        "gr_cg": gr_full.at[0:64], "cot_z": cot.at[0, 0:3, 0], "cot_x": cot.at[:, 0:2, 0],
        "cot_f": cot.at[:, 0, 0], "cot_c": cot.at[:, :, 0], "core": send_c, "far": out2,
        "near_x": send_c.at[:, 0:2], "near_z": out_z, "rot_h": rot.at[:, 0, 0:3],
        "rot_y": rot.at[:, 0:3], "s_z": s.at[:, 0, 0:3, 0], "s_x": s.at[:, 0:2, :, 0],
        "s_f": s.at[:, 0, :, 0], "s_c": s.at[:, :, :, 0],
    }
    for group, entry in sent.items():
        wait_bytes(send_sem, entry, bytes_like[group])
    assert len(sent) <= N_SENT and len(received) <= N_RECEIVED
    assert not any(size for _, size in received.values())


def body(activations, cotangent, eigenbasis, second_moment, factor, old_panel):
    vmem = pl.BlockSpec(memory_space=pltpu.VMEM)
    hbm = pl.BlockSpec(memory_space=pl.ANY)
    tile = (224, 128)
    half = (128, 256)
    part = (16, PANEL)
    scratch = [
        pltpu.VMEM((256, D), BF16),
        pltpu.VMEM((512, 256), F32),
        pltpu.VMEM((256, 256), BF16),
        pltpu.VMEM((224, 256), BF16),
        pltpu.VMEM((2, 4, 4) + tile, BF16),
        pltpu.VMEM((4, 4, 2, 112, 256), BF16),
        pltpu.VMEM((4, 4, 8, 256), F32),
        pltpu.VMEM((256, 256), F32),
        pltpu.VMEM((2,) + half, F32),
        pltpu.VMEM((2, 4, 4) + tile, BF16),
        pltpu.VMEM((2, 4, 4) + tile, BF16),
        pltpu.VMEM((2, 4) + tile, BF16),
        pltpu.VMEM((2, 4) + tile, BF16),
        pltpu.VMEM((2, 4) + tile, BF16),
        pltpu.VMEM((2, 4) + tile, BF16),
        pltpu.VMEM((2, 4) + tile, BF16),
        pltpu.VMEM((2, 4) + tile, BF16),
        pltpu.VMEM((2, 3) + tile, BF16),
        pltpu.VMEM((2, 3) + tile, BF16),
        pltpu.VMEM((2,) + tile, F32),
        pltpu.VMEM((2, 4, 4, 2) + half, BF16),
        pltpu.VMEM((256, 256), F32),
        pltpu.VMEM((4, 4, 2) + part, F32),
        pltpu.VMEM((4, 4) + part, F32),
        pltpu.VMEM((4, 4) + part, F32),
        pltpu.VMEM((4, 4) + part, F32),
        pltpu.VMEM((4,) + part, F32),
        pltpu.VMEM((4,) + part, F32),
        pltpu.VMEM((PANEL, PANEL), F32),
        pltpu.VMEM((64, PANEL), F32),
        pltpu.VMEM((64, PANEL), F32),
        pltpu.VMEM((4,) + part, F32),
        pltpu.VMEM(part, F32),
        pltpu.VMEM((4,) + part, F32),
        pltpu.VMEM(part, F32),
        pltpu.VMEM((4,) + part, F32),
        pltpu.VMEM(part, F32),
        pltpu.VMEM((4,) + part, F32),
        pltpu.VMEM((PANEL, PANEL), F32),
        pltpu.VMEM((PANEL, 2 * PANEL), F32),
        pltpu.SemaphoreType.DMA((N_SENT,)),
        pltpu.SemaphoreType.DMA((N_RECEIVED,)),
        pltpu.SemaphoreType.DMA((9,)),
    ]
    return pl.pallas_call(
        kernel,
        out_shape=(
            jax.ShapeDtypeStruct((256, 256), BF16),
            jax.ShapeDtypeStruct(part, F32),
        ),
        in_specs=[hbm] * 6,
        out_specs=(vmem, vmem),
        scratch_shapes=scratch,
        compiler_params=pltpu.CompilerParams(
            collective_id=0, has_side_effects=True, vmem_limit_bytes=60 * 1024 * 1024
        ),
    )(
        activations, cotangent, eigenbasis, second_moment, factor, old_panel.T
    )


def solution(mesh):
    return jax.shard_map(
        body,
        mesh=mesh,
        in_specs=(
            P("grp", "dev"),
            P("dev", "grp"),
            P("dev", None),
            P("dev", "grp"),
            P("grp", "dev"),
            P("dev", "grp"),
        ),
        out_specs=(P("dev", "grp"), P(("grp", "dev"), None)),
        check_vma=False,
    )
```
